512 devices in a mesh: seq: 64 (over y, z), head: 8 (over x, core).
Axes of the slice: x: 4, y: 4, z: 16, core: 2. Of those that a mesh axis runs over, the one named last changes fastest.
Arguments:
- queries: bfloat16 [8192, 4096], P(('seq', 'head')), may hold values from -16 to 16
- keys: bfloat16 [8192, 4096], P(('seq', 'head')), may hold values from -16 to 16
- values: bfloat16 [8192, 4096], P(('seq', 'head')), may hold values from -6 to 6
- out_grad: bfloat16 [8192, 4096], P(('seq', 'head')), may hold values from -6 to 6
Outputs:
- attended: bfloat16 [8192, 4096], P(('seq', 'head'))
- query_grad: bfloat16 [8192, 4096], P(('seq', 'head'))
- key_grad: bfloat16 [8192, 4096], P(('seq', 'head'))
- value_gradient_array: bfloat16 [8192, 4096], P(('seq', 'head'))
The draws below stay inside these ranges and needn't reach their ends.
All inputs are finite; a program needn't handle non-finite values.
Results may differ from the reference program's by a relative error of at most 0.034.
The reference program's roundings to bfloat16 on the way count: a program that leaves them out, or rounds other values in their place, can miss the bound.
Values may be sent and summed in bfloat16 or wider, within the bound.
A program may use at most 64 MiB of HBM per device.

```python
import jax
import jax.numpy as jnp
from jax import lax

H = 32
HD = 128
D = 4096
M = 256
PINV_ITERS = 6
TOKENS = 8192
SEG = 32


def base_field(key):
    noise_key, common_key = jax.random.split(jax.random.fold_in(key, 1), 2)
    noise = jax.random.normal(noise_key, (TOKENS, D), jnp.float32)
    common = jax.random.normal(common_key, (M, D), jnp.float32)
    return noise + jnp.repeat(common, SEG, axis=0)


def draw_queries(key, part):
    key = jax.random.fold_in(key, 11)
    field = base_field(key)
    return jnp.clip(field, -16.0, 16.0).astype(jnp.bfloat16)


def draw_keys(key, part):
    key = jax.random.fold_in(key, 23)
    field = base_field(key)
    return jnp.clip(field, -16.0, 16.0).astype(jnp.bfloat16)


def shard_levels(stream_key, dims, shards, least, high):
    gain, own = 1.0, jax.random.fold_in(stream_key, 6)
    for position, parts in shards:
        heights = jnp.exp(jax.random.uniform(jax.random.fold_in(own, position), (parts,), jnp.float32, least / len(shards), high / len(shards)))
        gain = gain * jnp.repeat(heights, dims[position] // parts).reshape([-1 if axis == position else 1 for axis in range(len(dims))])
    return gain


def normal_values(key, dims, scale, reach, shards=(), held_as=jnp.bfloat16):
    level = shard_levels(key, dims, shards, -0.22, 0.18) if shards else 1.0
    values = jax.random.normal(key, dims, jnp.float32) * scale * level
    return jnp.minimum(jnp.maximum(values, -reach), reach).astype(held_as)


def setup_inputs(seed: int = 0) -> dict:
    splits = jax.random.split(jax.random.key(seed), 5)
    return {
        "queries": draw_queries(jax.random.fold_in(splits[4], 71), 0),
        "keys": draw_keys(jax.random.fold_in(splits[4], 71), 0),
        "values": normal_values(splits[2], (TOKENS, D), 1.0, 6.0, ((0, 512),)),
        "out_grad": normal_values(splits[3], (TOKENS, D), 1.0, 6.0, ((0, 512),)),
    }


def exact_dot(left, right):
    return jnp.matmul(left, right, precision=lax.Precision.HIGHEST)

def newton_inverse(matrix):
    identity = jnp.eye(matrix.shape[0], dtype=matrix.dtype)
    factor = lax.stop_gradient(1.0 / jnp.max(lax.optimization_barrier(jnp.sum(matrix, axis=0))))
    iterate = matrix.T * factor
    for sweep_index in range(PINV_ITERS):
        product = exact_dot(matrix, iterate)
        inner_term = exact_dot(product, 7.0 * identity - product)
        inner_term = exact_dot(product, 15.0 * identity - inner_term)
        iterate = 0.25 * exact_dot(iterate, 13.0 * identity - inner_term)
    return iterate

def one_head(operands):
    query_cols, key_cols, value_cols, grad_cols = operands
    score_scale = HD ** (-0.5)
    landmark_q = (lax.optimization_barrier(jnp.sum(query_cols.reshape(M, SEG, HD), axis=1, dtype=jnp.float32)) / SEG).astype(jnp.bfloat16)
    landmark_k = (lax.optimization_barrier(jnp.sum(key_cols.reshape(M, SEG, HD), axis=1, dtype=jnp.float32)) / SEG).astype(jnp.bfloat16)
    token_prob = jax.nn.softmax(jnp.dot(query_cols, landmark_k.T, preferred_element_type=jnp.float32) * score_scale, axis=-1)
    token_probability_lowered = token_prob.astype(jnp.bfloat16)
    mark_prob = jax.nn.softmax(jnp.dot(landmark_q, landmark_k.T, preferred_element_type=jnp.float32) * score_scale, axis=-1)
    pseudo_inverse_matrix, pull_back = jax.vjp(newton_inverse, mark_prob)
    key_score = jnp.dot(landmark_q, key_cols.T, preferred_element_type=jnp.float32) * score_scale
    key_exp = jnp.exp(key_score - lax.optimization_barrier(jnp.max(key_score, axis=1, keepdims=True)))
    key_total = lax.optimization_barrier(jnp.sum(key_exp, axis=1))
    numerator = jnp.dot(key_exp.astype(jnp.bfloat16), value_cols, preferred_element_type=jnp.float32)
    landmark_value_rows = numerator / key_total[:, None]
    mixing_matrix = exact_dot(pseudo_inverse_matrix, landmark_value_rows)
    mixing_matrix_lowered = mixing_matrix.astype(jnp.bfloat16)
    attended = jnp.dot(token_probability_lowered, mixing_matrix_lowered, preferred_element_type=jnp.float32).astype(jnp.bfloat16)
    token_grad = jnp.dot(grad_cols, mixing_matrix_lowered.T, preferred_element_type=jnp.float32)
    mixing_matrix_gradient = jnp.dot(token_probability_lowered.T, grad_cols, preferred_element_type=jnp.float32)
    token_score_gradient = (token_prob * (token_grad - lax.optimization_barrier(jnp.sum(token_grad * token_prob, axis=1, keepdims=True)))).astype(jnp.bfloat16)
    direct_qgrad = jnp.dot(token_score_gradient, landmark_k, preferred_element_type=jnp.float32) * score_scale
    mark_kgrad_f = jnp.dot(token_score_gradient.T, query_cols, preferred_element_type=jnp.float32) * score_scale
    pseudo_inverse_gradient = exact_dot(mixing_matrix_gradient, landmark_value_rows.T)
    landmark_value_gradient = exact_dot(pseudo_inverse_matrix.T, mixing_matrix_gradient)
    mark_grad, = pull_back(pseudo_inverse_gradient)
    mark_sgrad = mark_prob * (mark_grad - lax.optimization_barrier(jnp.sum(mark_grad * mark_prob, axis=1, keepdims=True)))
    mark_qgrad_a = exact_dot(mark_sgrad, landmark_k.astype(jnp.float32)) * score_scale
    mark_kgrad_a = exact_dot(mark_sgrad.T, landmark_q.astype(jnp.float32)) * score_scale
    landmark_value_lowered = landmark_value_gradient.astype(jnp.bfloat16)
    key_prob = key_exp / key_total[:, None]
    key_probability_lowered = key_prob.astype(jnp.bfloat16)
    value_gradient_array = jnp.dot(key_probability_lowered.T, landmark_value_lowered, preferred_element_type=jnp.float32)
    key_direct_gradient = jnp.dot(landmark_value_lowered, value_cols.T, preferred_element_type=jnp.float32)
    row_total = lax.optimization_barrier(jnp.sum(key_prob * key_direct_gradient, axis=1, keepdims=True))
    key_score_gradient = (key_prob * (key_direct_gradient - row_total)).astype(jnp.bfloat16)
    direct_kgrad = jnp.dot(key_score_gradient.T, landmark_q, preferred_element_type=jnp.float32) * score_scale
    mark_qgrad_b = jnp.dot(key_score_gradient, key_cols, preferred_element_type=jnp.float32) * score_scale
    query_grad = direct_qgrad + jnp.repeat((mark_qgrad_a + mark_qgrad_b) / SEG, SEG, axis=0)
    key_grad = direct_kgrad + jnp.repeat((mark_kgrad_a + mark_kgrad_f) / SEG, SEG, axis=0)
    return (attended, query_grad.astype(jnp.bfloat16), key_grad.astype(jnp.bfloat16), value_gradient_array.astype(jnp.bfloat16))

def split_heads(matrix):
    return jnp.transpose(matrix.reshape(TOKENS, H, HD), (1, 0, 2))

def join_heads(stacked):
    return jnp.transpose(stacked, (1, 0, 2)).reshape(TOKENS, D)

def reference(queries, keys, values, out_grad):
    results = lax.map(one_head, (split_heads(queries), split_heads(keys), split_heads(values), split_heads(out_grad)))
    return (join_heads(results[0]), join_heads(results[1]), join_heads(results[2]), join_heads(results[3]))
```

```python
import functools

import jax
import jax.numpy as jnp
from jax import lax
from jax.experimental import pallas as pl
from jax.experimental.pallas import tpu as pltpu
from jax.sharding import PartitionSpec as P

MESH = pl.DeviceIdType.MESH
F32, BF16 = jnp.float32, jnp.bfloat16

NZ = 16
PLANE = 32
HEADS = 8
ROWS = 16
HD = 128
D = PLANE * HD
TOK = PLANE * ROWS
SEG = 32
OWN = TOK // SEG
M = NZ * OWN
SLAB = HD // NZ
ITERS = 6
SCALE = HD ** (-0.5)

X_QK, X_VG, X_MARK, X_PART, X_SUM, X_AV, X_GRAD, X_OUT = range(8)


def dot(left, right):
    return lax.dot_general(left, right, (((1,), (0,)), ((), ())), preferred_element_type=F32)


def dot_nt(left, right):
    return lax.dot_general(left, right, (((1,), (1,)), ((), ())), preferred_element_type=F32)


def split(x):
    high = x.astype(BF16)
    return high, (x - high.astype(F32)).astype(BF16)


def mul(left, right, product=dot):
    return product(left[0], right[0]) + (product(left[0], right[1]) + product(left[1], right[0]))


def kernel(
    q_ref, k_ref, v_ref, g_ref, av_ref, qk_ref,
    qk_in, vg_in, qk, vg, mark_out, marks, part_out, parts, sum_out, sums, av_out, grad_out, grads, qk_out,
    prob, low, kexp, trans, direct, square, saved, load_sem, send_sem, recv_sem,
):
    seq, head = lax.axis_index("seq"), lax.axis_index("head")
    y, z = seq // NZ, seq % NZ
    me = y * HEADS + head

    def plane_peer(rank):
        return (rank // HEADS * NZ + z, rank % HEADS)

    def line_peer(rank):
        return (y * NZ + rank, head)

    loads = [
        pltpu.make_async_copy(source, target, load_sem.at[index])
        for index, (source, target) in enumerate(
            ((q_ref, qk_in.at[0]), (k_ref, qk_in.at[1]), (v_ref, vg_in.at[0]), (g_ref, vg_in.at[1]))
        )
    ]
    for load in loads:
        load.start()

    barrier = pltpu.get_barrier_semaphore()

    @pl.loop(1, PLANE)
    def _(step):
        pl.semaphore_signal(barrier, inc=1, device_id=plane_peer((me + step) % PLANE), device_id_type=MESH)

    @pl.loop(1, NZ)
    def _(step):
        pl.semaphore_signal(barrier, inc=1, device_id=line_peer((z + step) % NZ), device_id_type=MESH)

    pl.semaphore_wait(barrier, PLANE - 1 + NZ - 1)

    def send(source, target, index, peer):
        pltpu.make_async_remote_copy(
            src_ref=source, dst_ref=target, send_sem=send_sem.at[index], recv_sem=recv_sem.at[index],
            device_id=peer, device_id_type=MESH,
        ).start()

    def columns(rank):
        return pl.ds(pl.multiple_of(rank * HD, HD), HD)

    def rows(rank, count):
        return pl.ds(pl.multiple_of(rank * count, count), count)

    def scatter_heads(source, target, index):
        @pl.loop(1, PLANE)
        def _(step):
            peer = (me + step) % PLANE
            send(source.at[:, :, columns(peer)], target.at[:, rows(me, ROWS), :], index, plane_peer(peer))

        target[:, rows(me, ROWS), :] = source[:, :, columns(me)]

    def gather_heads(source, target, index):
        @pl.loop(1, PLANE)
        def _(step):
            peer = (me + step) % PLANE
            send(source.at[:, rows(peer, ROWS), :], target.at[:, :, columns(me)], index, plane_peer(peer))

        own = pltpu.make_async_copy(source.at[:, rows(me, ROWS), :], target.at[:, :, columns(me)], load_sem.at[0])
        own.start()
        own.wait()

    def over_line(source, target, index):
        @pl.loop(1, NZ)
        def _(step):
            peer = (z + step) % NZ
            send(source(peer), target.at[z], index, line_peer(peer))

    def arrived(span, index):
        pltpu.make_async_copy(span, span, recv_sem.at[index]).wait()

    def left(span, index):
        pltpu.make_async_copy(span, span, send_sem.at[index]).wait()

    loads[0].wait()
    loads[1].wait()
    scatter_heads(qk_in, qk, X_QK)
    loads[2].wait()
    loads[3].wait()
    scatter_heads(vg_in, vg, X_VG)
    plane_span = qk.at[:, pl.ds(0, TOK - ROWS), :]
    arrived(plane_span, X_QK)

    for index in range(2):
        summed = jnp.sum(qk[index].astype(F32).reshape(OWN, SEG, HD), axis=1)
        mark_out[index] = (summed * (1.0 / SEG)).astype(BF16)
    over_line(lambda peer: mark_out, marks, X_MARK)
    marks[z] = mark_out[...]
    for index in range(2):
        trans[index] = qk[index].T
    arrived(plane_span, X_VG)
    for index in range(2):
        trans[2 + index] = vg[index].T
    arrived(marks.at[pl.ds(0, NZ - 1)], X_MARK)
    mark_q = marks[:, 0].reshape(M, HD)
    mark_k = marks[:, 1].reshape(M, HD)

    scores = dot_nt(qk[0], mark_k)
    top = jnp.max(scores, axis=1, keepdims=True)
    exps = jnp.exp((scores - top) * SCALE)
    token_prob = exps * (1.0 / jnp.sum(exps, axis=1, keepdims=True))
    prob[...] = token_prob
    token_low = token_prob.astype(BF16)
    low[...] = token_low
    mixing_part = dot(trans[3], token_low)

    scores = dot_nt(qk[1], mark_q)
    key_top = jnp.max(scores, axis=0, keepdims=True)
    exps = jnp.exp((scores - key_top) * SCALE)
    kexp[...] = exps
    key_sum = jnp.sum(exps, axis=0, keepdims=True)
    value_part = dot(trans[2], exps.astype(BF16))
    part_out[:, 0:SLAB, :] = value_part.reshape(NZ, SLAB, M)
    part_out[:, SLAB : 2 * SLAB, :] = mixing_part.reshape(NZ, SLAB, M)
    stats = jnp.concatenate([jnp.broadcast_to(key_top, (4, M)), jnp.broadcast_to(key_sum, (4, M))], axis=0)
    part_out[:, 2 * SLAB : 3 * SLAB, :] = jnp.broadcast_to(stats[None], (NZ, SLAB, M))
    over_line(lambda peer: part_out.at[peer], parts, X_PART)
    parts[z] = part_out[z]

    scores = dot_nt(mark_q, mark_k)
    exps = jnp.exp((scores - jnp.max(scores, axis=1, keepdims=True)) * SCALE)
    mark_prob = exps * (1.0 / jnp.sum(exps, axis=1, keepdims=True))
    square[0] = mark_prob
    factor = 1.0 / jnp.max(jnp.sum(mark_prob, axis=0, keepdims=True))
    square[1] = mark_prob.T * factor

    def keep(step, slot, value):
        saved[step, slot], saved[step, slot + 1] = split(value)

    def kept(step, slot):
        return saved[step, slot], saved[step, slot + 1]

    mark_split = split(mark_prob)
    keep(ITERS, 8, mark_prob.T)

    @pl.loop(0, ITERS)
    def _(step):
        iterate = square[1]
        keep(step, 0, iterate)
        keep(step, 2, iterate.T)
        part = kept(step, 0)
        product = mul(split(square[0]), part)
        keep(step, 4, product)
        product_split = kept(step, 4)
        first = 7.0 * product - mul(product_split, product_split)
        keep(step, 6, first)
        second = 15.0 * product - mul(product_split, kept(step, 6))
        keep(step, 8, second)
        square[1] = 3.25 * iterate - 0.25 * mul(part, kept(step, 8))

    keep(ITERS, 0, square[1])

    arrived(parts.at[pl.ds(0, NZ - 1)], X_PART)
    tops = [parts[peer, 2 * SLAB : 2 * SLAB + 1, :] for peer in range(NZ)]
    highest = functools.reduce(jnp.maximum, tops)
    total, values, mixing_grad = 0.0, 0.0, 0.0
    for peer in range(NZ):
        weight = jnp.exp((tops[peer] - highest) * SCALE)
        total = total + weight * parts[peer, 2 * SLAB + 4 : 2 * SLAB + 5, :]
        values = values + weight * parts[peer, 0:SLAB, :]
        mixing_grad = mixing_grad + parts[peer, SLAB : 2 * SLAB, :]
    sum_out[0:SLAB, :] = values / total
    sum_out[SLAB : 2 * SLAB, :] = mixing_grad
    over_line(lambda peer: sum_out, sums, X_SUM)
    sums[z] = sum_out[...]
    key_prob = kexp[...] * (jnp.exp((key_top - highest) * SCALE) / total)
    kexp[...] = key_prob
    arrived(sums.at[pl.ds(0, NZ - 1)], X_SUM)
    values = sums[:, 0:SLAB, :].reshape(HD, M)
    mixing_grad = sums[:, SLAB : 2 * SLAB, :].reshape(HD, M)
    values_split, grad_split = split(values), split(mixing_grad)
    inverse = kept(ITERS, 0)
    mixing_low = mul(values_split, inverse, dot_nt).astype(BF16)
    lv_low = mul(grad_split, inverse).astype(BF16)
    square[1] = mul(split(mixing_grad.T), values_split)
    square[2] = jnp.zeros((M, M), F32)

    token_prob = prob[...]
    av_out[0] = dot_nt(low[...], mixing_low).astype(BF16)
    token_grad = dot(vg[1], mixing_low)
    dots = jnp.sum(token_grad * token_prob, axis=1, keepdims=True)
    token_sgrad = (token_prob * (token_grad - dots)).astype(BF16)
    direct[0] = dot(token_sgrad, mark_k) * SCALE
    grad_out[0] = (dot(trans[0], token_sgrad) * SCALE).T
    key_prob = kexp[...]
    av_out[1] = dot_nt(key_prob.astype(BF16), lv_low).astype(BF16)
    row_total = jnp.sum(lv_low.astype(F32) * values, axis=0, keepdims=True)
    key_dgrad = dot(vg[0], lv_low)
    key_sgrad = (key_prob * (key_dgrad - row_total)).astype(BF16)
    direct[1] = dot(key_sgrad, mark_q) * SCALE
    grad_out[1] = (dot(trans[1], key_sgrad) * SCALE).T
    over_line(lambda peer: grad_out.at[:, rows(peer, OWN), :], grads, X_GRAD)
    grads[z] = grad_out[:, rows(z, OWN), :]
    gather_heads(av_out, av_ref, X_AV)

    @pl.loop(0, ITERS)
    def _(back):
        step = ITERS - 1 - back
        out_grad = square[1]
        out_split = split(out_grad)
        second_grad = -0.25 * mul(kept(step, 2), out_split)
        iterate_grad = 3.25 * out_grad - 0.25 * mul(out_split, kept(step, 8))
        second_split = split(second_grad)
        product_split = kept(step, 4)
        product_grad = 15.0 * second_grad - mul(second_split, kept(step, 6))
        first_grad = -mul(product_split, second_split)
        first_split = split(first_grad)
        product_grad = product_grad + 7.0 * first_grad
        product_grad = product_grad - (mul(first_split, product_split) + mul(product_split, first_split))
        product_grad_split = split(product_grad)
        square[2] += mul(product_grad_split, kept(step, 0), dot_nt)
        square[1] = iterate_grad + mul(kept(ITERS, 8), product_grad_split)

    mark_grad = square[2] + square[1].T * factor
    mark_prob = square[0]
    mark_sgrad = mark_prob * (mark_grad - jnp.sum(mark_grad * mark_prob, axis=1, keepdims=True))
    square[1] = mark_sgrad
    square[2] = mark_sgrad.T
    arrived(grads.at[pl.ds(0, NZ - 1)], X_GRAD)
    from_query, from_key = split(square[1, rows(z, OWN), :]), split(square[2, rows(z, OWN), :])
    query_marks = (dot(from_query[0], mark_k) + dot(from_query[1], mark_k)) * SCALE
    key_marks = (dot(from_key[0], mark_q) + dot(from_key[1], mark_q)) * SCALE
    for peer in range(NZ):
        query_marks = query_marks + grads[peer, 1]
        key_marks = key_marks + grads[peer, 0]
    for index, total in ((0, query_marks), (1, key_marks)):
        spread = direct[index].reshape(OWN, SEG, HD) + (total * (1.0 / SEG))[:, None, :]
        qk_out[index] = spread.reshape(TOK, HD).astype(BF16)
    gather_heads(qk_out, qk_ref, X_OUT)

    out_span = av_ref.at[:, :, pl.ds(0, D - HD)]
    arrived(out_span, X_AV)
    arrived(out_span, X_OUT)
    for index in (X_QK, X_VG, X_AV, X_OUT):
        left(plane_span, index)
    left(marks.at[pl.ds(0, NZ - 1)], X_MARK)
    left(parts.at[pl.ds(0, NZ - 1)], X_PART)
    left(sums.at[pl.ds(0, NZ - 1)], X_SUM)
    left(grads.at[pl.ds(0, NZ - 1)], X_GRAD)


def body(queries, keys, values, out_grad):
    pair = jax.ShapeDtypeStruct((2, ROWS, D), BF16)
    anywhere = pl.BlockSpec(memory_space=pl.ANY)
    av, qk = pl.pallas_call(
        kernel,
        out_shape=(pair, pair),
        in_specs=[anywhere] * 4,
        out_specs=(anywhere, anywhere),
        scratch_shapes=[
            pltpu.VMEM((2, ROWS, D), BF16),
            pltpu.VMEM((2, ROWS, D), BF16),
            pltpu.VMEM((2, TOK, HD), BF16),
            pltpu.VMEM((2, TOK, HD), BF16),
            pltpu.VMEM((2, OWN, HD), BF16),
            pltpu.VMEM((NZ, 2, OWN, HD), BF16),
            pltpu.VMEM((NZ, 3 * SLAB, M), F32),
            pltpu.VMEM((NZ, 3 * SLAB, M), F32),
            pltpu.VMEM((2 * SLAB, M), F32),
            pltpu.VMEM((NZ, 2 * SLAB, M), F32),
            pltpu.VMEM((2, TOK, HD), BF16),
            pltpu.VMEM((2, M, HD), F32),
            pltpu.VMEM((NZ, 2, OWN, HD), F32),
            pltpu.VMEM((2, TOK, HD), BF16),
            pltpu.VMEM((TOK, M), F32),
            pltpu.VMEM((TOK, M), BF16),
            pltpu.VMEM((TOK, M), F32),
            pltpu.VMEM((4, HD, TOK), BF16),
            pltpu.VMEM((2, TOK, HD), F32),
            pltpu.VMEM((3, M, M), F32),
            pltpu.VMEM((ITERS + 1, 10, M, M), BF16),
            pltpu.SemaphoreType.DMA((4,)),
            pltpu.SemaphoreType.DMA((8,)),
            pltpu.SemaphoreType.DMA((8,)),
        ],
        compiler_params=pltpu.CompilerParams(
            collective_id=0, has_side_effects=True, vmem_limit_bytes=48 * 1024 * 1024
        ),
    )(queries, keys, values, out_grad)
    return av[0], qk[0], qk[1], av[1]


def solution(mesh):
    spec = P(("seq", "head"), None)
    return jax.shard_map(body, mesh=mesh, in_specs=(spec,) * 4, out_specs=(spec,) * 4, check_vma=False)
```

```python
import functools

import jax
import jax.numpy as jnp
from jax import lax
from jax.experimental import pallas as pl
from jax.experimental.pallas import tpu as pltpu
from jax.sharding import PartitionSpec as P

MESH = pl.DeviceIdType.MESH
F32, BF16 = jnp.float32, jnp.bfloat16

NZ = 16
PLANE = 32
HEADS = 8
ROWS = 16
HD = 128
D = PLANE * HD
TOK = PLANE * ROWS
SEG = 32
OWN = TOK // SEG
M = NZ * OWN
SLAB = HD // NZ
ITERS = 6
SCALE = HD ** (-0.5)


def away(step, size):
    return min(step % size, -step % size)


NY, NX = 4, 4
PLANE_STEPS = sorted(
    ((i, j, k) for i in range(NY) for j in range(NX) for k in range(2) if i or j or k),
    key=lambda step: -away(step[0], NY) - away(step[1], NX),
)
LINE_STEPS = sorted(range(1, NZ), key=lambda step: -away(step, NZ))

X_QK, X_VG, X_MARK, X_PART, X_SUM, X_AV, X_GRAD, X_OUT, X_STAT = range(9)


def dot(left, right):
    return lax.dot_general(left, right, (((1,), (0,)), ((), ())), preferred_element_type=F32)


def dot_nt(left, right):
    return lax.dot_general(left, right, (((1,), (1,)), ((), ())), preferred_element_type=F32)


def split(x):
    high = x.astype(BF16)
    return high, (x - high.astype(F32)).astype(BF16)


def mul(left, right, product=dot):
    return product(left[0], right[0]) + (product(left[0], right[1]) + product(left[1], right[0]))


def kernel(
    q_ref, k_ref, v_ref, g_ref, av_ref, qk_ref,
    qk_in, vg_in, qk, vg, mark_out, marks, part_out, parts, stat_out, stats, sum_out, sums, av_out, grad_out, grads, qk_out,
    prob, low, kexp, trans, direct, square, saved, load_sem, send_sem, recv_sem,
):
    seq, head = lax.axis_index("seq"), lax.axis_index("head")
    y, z = seq // NZ, seq % NZ
    me = y * HEADS + head

    def plane_peer(rank):
        return (rank // HEADS * NZ + z, rank % HEADS)

    def line_peer(rank):
        return (y * NZ + rank, head)

    loads = [
        pltpu.make_async_copy(source, target, load_sem.at[index])
        for index, (source, target) in enumerate(
            ((q_ref, qk_in.at[0]), (k_ref, qk_in.at[1]), (v_ref, vg_in.at[0]), (g_ref, vg_in.at[1]))
        )
    ]
    for load in loads:
        load.start()

    barrier = pltpu.get_barrier_semaphore()

    @pl.loop(1, PLANE)
    def _(step):
        pl.semaphore_signal(barrier, inc=1, device_id=plane_peer((me + step) % PLANE), device_id_type=MESH)

    @pl.loop(1, NZ)
    def _(step):
        pl.semaphore_signal(barrier, inc=1, device_id=line_peer((z + step) % NZ), device_id_type=MESH)

    pl.semaphore_wait(barrier, PLANE - 1 + NZ - 1)

    def send(source, target, index, peer):
        pltpu.make_async_remote_copy(
            src_ref=source, dst_ref=target, send_sem=send_sem.at[index], recv_sem=recv_sem.at[index],
            device_id=peer, device_id_type=MESH,
        ).start()

    def columns(rank):
        return pl.ds(pl.multiple_of(rank * HD, HD), HD)

    def rows(rank, count):
        return pl.ds(pl.multiple_of(rank * count, count), count)

    def plane_ranks():
        for i, j, k in PLANE_STEPS:
            yield (y + i) % NY * HEADS + (head // 2 + j) % NX * 2 + (head + k) % 2

    def scatter_heads(source, target, index):
        for peer in plane_ranks():
            send(source.at[:, :, columns(peer)], target.at[:, rows(me, ROWS), :], index, plane_peer(peer))

        target[:, rows(me, ROWS), :] = source[:, :, columns(me)]

    def gather_heads(source, target, index):
        for peer in plane_ranks():
            send(source.at[:, rows(peer, ROWS), :], target.at[:, :, columns(me)], index, plane_peer(peer))

        own = pltpu.make_async_copy(source.at[:, rows(me, ROWS), :], target.at[:, :, columns(me)], load_sem.at[0])
        own.start()
        own.wait()

    def over_line(source, target, index):
        for step in LINE_STEPS:
            peer = (z + step) % NZ
            send(source(peer), target.at[z], index, line_peer(peer))

    def arrived(span, index):
        pltpu.make_async_copy(span, span, recv_sem.at[index]).wait()

    def left(span, index):
        pltpu.make_async_copy(span, span, send_sem.at[index]).wait()

    loads[0].wait()
    loads[1].wait()
    scatter_heads(qk_in, qk, X_QK)
    plane_span = qk.at[:, pl.ds(0, TOK - ROWS), :]
    arrived(plane_span, X_QK)

    for index in range(2):
        summed = jnp.sum(qk[index].astype(F32).reshape(OWN, SEG, HD), axis=1)
        mark_out[index] = (summed * (1.0 / SEG)).astype(BF16)
    over_line(lambda peer: mark_out, marks, X_MARK)
    marks[z] = mark_out[...]
    loads[2].wait()
    loads[3].wait()
    scatter_heads(vg_in, vg, X_VG)
    for index in range(2):
        trans[index] = qk[index].T
    arrived(plane_span, X_VG)
    for index in range(2):
        trans[2 + index] = vg[index].T
    arrived(marks.at[pl.ds(0, NZ - 1)], X_MARK)
    mark_q = marks[:, 0].reshape(M, HD)
    mark_k = marks[:, 1].reshape(M, HD)

    scores = dot_nt(qk[1], mark_q)
    key_top = jnp.max(scores, axis=0, keepdims=True)
    exps = jnp.exp((scores - key_top) * SCALE)
    kexp[...] = exps
    key_sum = jnp.sum(exps, axis=0, keepdims=True)
    stat_out[0:1, :] = key_top
    stat_out[1:2, :] = key_sum
    over_line(lambda peer: stat_out, stats, X_STAT)
    stats[z] = stat_out[...]
    value_part = dot(trans[2], exps.astype(BF16))
    scores = dot_nt(qk[0], mark_k)
    top = jnp.max(scores, axis=1, keepdims=True)
    exps = jnp.exp((scores - top) * SCALE)
    token_prob = exps * (1.0 / jnp.sum(exps, axis=1, keepdims=True))
    prob[...] = token_prob
    token_low = token_prob.astype(BF16)
    low[...] = token_low
    mixing_part = dot(trans[3], token_low)
    pair = [value_part.reshape(NZ, SLAB, M), mixing_part.reshape(NZ, SLAB, M)]
    part_out[...] = jnp.concatenate(pair, axis=1).astype(BF16)
    over_line(lambda peer: part_out.at[peer], parts, X_PART)
    parts[z] = part_out[z]

    scores = dot_nt(mark_q, mark_k)
    exps = jnp.exp((scores - jnp.max(scores, axis=1, keepdims=True)) * SCALE)
    mark_prob = exps * (1.0 / jnp.sum(exps, axis=1, keepdims=True))
    square[0] = mark_prob
    factor = 1.0 / jnp.max(jnp.sum(mark_prob, axis=0, keepdims=True))
    square[1] = mark_prob.T * factor

    def keep(step, slot, value):
        saved[step, slot], saved[step, slot + 1] = split(value)

    def kept(step, slot):
        return saved[step, slot], saved[step, slot + 1]

    keep(ITERS, 8, mark_prob.T)

    @pl.loop(0, ITERS)
    def _(step):
        iterate = square[1]
        keep(step, 0, iterate)
        keep(step, 2, iterate.T)
        part = kept(step, 0)
        product = mul(split(square[0]), part)
        keep(step, 4, product)
        product_split = kept(step, 4)
        first = 7.0 * product - mul(product_split, product_split)
        keep(step, 6, first)
        second = 15.0 * product - mul(product_split, kept(step, 6))
        keep(step, 8, second)
        square[1] = 3.25 * iterate - 0.25 * mul(part, kept(step, 8))

    keep(ITERS, 0, square[1])

    arrived(stats.at[pl.ds(0, NZ - 1)], X_STAT)
    arrived(parts.at[pl.ds(0, NZ - 1)], X_PART)
    tops = [stats[peer, 0:1, :] for peer in range(NZ)]
    highest = functools.reduce(jnp.maximum, tops)
    total, values, mixing_grad = 0.0, 0.0, 0.0
    for peer in range(NZ):
        weight = jnp.exp((tops[peer] - highest) * SCALE)
        total = total + weight * stats[peer, 1:2, :]
        part = parts[peer].astype(F32)
        values = values + weight * part[0:SLAB]
        mixing_grad = mixing_grad + part[SLAB : 2 * SLAB]
    sum_out[...] = jnp.concatenate([values / total, mixing_grad], axis=0).astype(BF16)
    over_line(lambda peer: sum_out, sums, X_SUM)
    sums[z] = sum_out[...]
    key_prob = kexp[...] * (jnp.exp((key_top - highest) * SCALE) / total)
    kexp[...] = key_prob
    arrived(sums.at[pl.ds(0, NZ - 1)], X_SUM)
    both = sums[...].astype(F32)
    values = both[:, 0:SLAB, :].reshape(HD, M)
    mixing_grad = both[:, SLAB : 2 * SLAB, :].reshape(HD, M)
    values_split, grad_split = split(values), split(mixing_grad)
    inverse = kept(ITERS, 0)
    mixing_low = mul(values_split, inverse, dot_nt).astype(BF16)
    lv_low = mul(grad_split, inverse).astype(BF16)
    square[1] = mul(split(mixing_grad.T), values_split)
    square[2] = jnp.zeros((M, M), F32)

    token_prob = prob[...]
    av_out[0] = dot_nt(low[...], mixing_low).astype(BF16)
    token_grad = dot(vg[1], mixing_low)
    dots = jnp.sum(token_grad * token_prob, axis=1, keepdims=True)
    token_sgrad = (token_prob * (token_grad - dots)).astype(BF16)
    direct[0] = dot(token_sgrad, mark_k) * SCALE
    grad_out[0] = (dot(trans[0], token_sgrad) * SCALE).T.astype(BF16)
    key_prob = kexp[...]
    av_out[1] = dot_nt(key_prob.astype(BF16), lv_low).astype(BF16)
    row_total = jnp.sum(lv_low.astype(F32) * values, axis=0, keepdims=True)
    key_dgrad = dot(vg[0], lv_low)
    key_sgrad = (key_prob * (key_dgrad - row_total)).astype(BF16)
    direct[1] = dot(key_sgrad, mark_q) * SCALE
    grad_out[1] = (dot(trans[1], key_sgrad) * SCALE).T.astype(BF16)
    over_line(lambda peer: grad_out.at[:, rows(peer, OWN), :], grads, X_GRAD)
    grads[z] = grad_out[:, rows(z, OWN), :]
    gather_heads(av_out, av_ref, X_AV)

    square[3] = -0.25 * mul(kept(ITERS - 1, 2), split(square[1]))

    @pl.loop(0, ITERS)
    def _(back):
        step = ITERS - 1 - back
        before = jnp.maximum(step - 1, 0)
        second_grad = square[3]
        second_split = split(second_grad)
        product_split = kept(step, 4)
        first_split = kept(step, 6)
        through = split(mul(product_split, second_split))
        product_grad = 15.0 * second_grad - (mul(second_split, first_split) + mul(first_split, second_split))
        product_grad = split(product_grad + mul(through, product_split))
        out_grad = square[1]
        out_grad = 3.25 * out_grad - 0.25 * mul(split(out_grad), kept(step, 8))
        earlier = mul(kept(before, 2), split(out_grad))
        square[3] = -0.25 * (earlier + mul(kept(before, 4), product_grad))
        square[1] = out_grad + mul(kept(ITERS, 8), product_grad)
        square[2] += mul(product_grad, kept(step, 0), dot_nt)

    mark_grad = square[2] + square[1].T * factor
    mark_prob = square[0]
    mark_sgrad = mark_prob * (mark_grad - jnp.sum(mark_grad * mark_prob, axis=1, keepdims=True))
    square[1] = mark_sgrad
    square[2] = mark_sgrad.T
    arrived(grads.at[pl.ds(0, NZ - 1)], X_GRAD)
    from_query, from_key = split(square[1, rows(z, OWN), :]), split(square[2, rows(z, OWN), :])
    query_marks = (dot(from_query[0], mark_k) + dot(from_query[1], mark_k)) * SCALE
    key_marks = (dot(from_key[0], mark_q) + dot(from_key[1], mark_q)) * SCALE
    for peer in range(NZ):
        query_marks = query_marks + grads[peer, 1].astype(F32)
        key_marks = key_marks + grads[peer, 0].astype(F32)
    for index, total in ((0, query_marks), (1, key_marks)):
        spread = direct[index].reshape(OWN, SEG, HD) + (total * (1.0 / SEG))[:, None, :]
        qk_out[index] = spread.reshape(TOK, HD).astype(BF16)
    gather_heads(qk_out, qk_ref, X_OUT)

    out_span = av_ref.at[:, :, pl.ds(0, D - HD)]
    arrived(out_span, X_AV)
    arrived(out_span, X_OUT)
    for index in (X_QK, X_VG, X_AV, X_OUT):
        left(plane_span, index)
    left(marks.at[pl.ds(0, NZ - 1)], X_MARK)
    left(stats.at[pl.ds(0, NZ - 1)], X_STAT); left(parts.at[pl.ds(0, NZ - 1)], X_PART)
    left(sums.at[pl.ds(0, NZ - 1)], X_SUM)
    left(grads.at[pl.ds(0, NZ - 1)], X_GRAD)


def body(queries, keys, values, out_grad):
    pair = jax.ShapeDtypeStruct((2, ROWS, D), BF16)
    anywhere = pl.BlockSpec(memory_space=pl.ANY)
    av, qk = pl.pallas_call(
        kernel,
        out_shape=(pair, pair),
        in_specs=[anywhere] * 4,
        out_specs=(anywhere, anywhere),
        scratch_shapes=[
            pltpu.VMEM((2, ROWS, D), BF16),
            pltpu.VMEM((2, ROWS, D), BF16),
            pltpu.VMEM((2, TOK, HD), BF16),
            pltpu.VMEM((2, TOK, HD), BF16),
            pltpu.VMEM((2, OWN, HD), BF16),
            pltpu.VMEM((NZ, 2, OWN, HD), BF16),
            pltpu.VMEM((NZ, 2 * SLAB, M), BF16),
            pltpu.VMEM((NZ, 2 * SLAB, M), BF16),
            pltpu.VMEM((2, M), F32),
            pltpu.VMEM((NZ, 2, M), F32),
            pltpu.VMEM((2 * SLAB, M), BF16),
            pltpu.VMEM((NZ, 2 * SLAB, M), BF16),
            pltpu.VMEM((2, TOK, HD), BF16),
            pltpu.VMEM((2, M, HD), BF16),
            pltpu.VMEM((NZ, 2, OWN, HD), BF16),
            pltpu.VMEM((2, TOK, HD), BF16),
            pltpu.VMEM((TOK, M), F32),
            pltpu.VMEM((TOK, M), BF16),
            pltpu.VMEM((TOK, M), F32),
            pltpu.VMEM((4, HD, TOK), BF16),
            pltpu.VMEM((2, TOK, HD), F32),
            pltpu.VMEM((4, M, M), F32),
            pltpu.VMEM((ITERS + 1, 10, M, M), BF16),
            pltpu.SemaphoreType.DMA((4,)),
            pltpu.SemaphoreType.DMA((9,)),
            pltpu.SemaphoreType.DMA((9,)),
        ],
        compiler_params=pltpu.CompilerParams(
            collective_id=0, has_side_effects=True, vmem_limit_bytes=63 * 1024 * 1024
        ),
    )(queries, keys, values, out_grad)
    return av[0], qk[0], qk[1], av[1]


def solution(mesh):
    spec = P(("seq", "head"), None)
    return jax.shard_map(body, mesh=mesh, in_specs=(spec,) * 4, out_specs=(spec,) * 4, check_vma=False)
```

```python
import functools

import jax
import jax.numpy as jnp
from jax import lax
from jax.experimental import pallas as pl
from jax.experimental.pallas import tpu as pltpu
from jax.sharding import PartitionSpec as P

MESH = pl.DeviceIdType.MESH
F32, BF16 = jnp.float32, jnp.bfloat16

NZ = 16
PLANE = 32
HEADS = 8
ROWS = 16
HD = 128
D = PLANE * HD
TOK = PLANE * ROWS
SEG = 32
OWN = TOK // SEG
M = NZ * OWN
SLAB = HD // NZ
ITERS = 6
SCALE = HD ** (-0.5)


def away(step, size):
    return min(step % size, -step % size)


NY, NX = 4, 4
PLANE_STEPS = sorted(
    ((i, j, k) for i in range(NY) for j in range(NX) for k in range(2) if i or j or k),
    key=lambda step: -away(step[0], NY) - away(step[1], NX),
)
CHIP_STEPS = [(i, j) for i, j, k in PLANE_STEPS if k == 0]
LINE_STEPS = sorted(range(1, NZ), key=lambda step: -away(step, NZ))

X_QK, X_VG, X_MARK, X_PART, X_SUM, X_AV, X_GRAD, X_OUT, X_STAT = range(9)


def dot(left, right):
    return lax.dot_general(left, right, (((1,), (0,)), ((), ())), preferred_element_type=F32)


def dot_nt(left, right):
    return lax.dot_general(left, right, (((1,), (1,)), ((), ())), preferred_element_type=F32)


def split(x):
    high = x.astype(BF16)
    return high, (x - high.astype(F32)).astype(BF16)


def mul(left, right, product=dot):
    return product(left[0], right[0]) + (product(left[0], right[1]) + product(left[1], right[0]))


def kernel(
    q_ref, k_ref, v_ref, g_ref, av_ref, qk_ref,
    qk_in, vg_in, qk, vg, mark_out, marks, part_out, parts, stat_out, stats, sum_out, sums, av_out, grad_out, grads, qk_out,
    prob, low, kexp, trans, direct, square, saved, sync_sem, load_sem, send_sem, recv_sem,
):
    seq, head = lax.axis_index("seq"), lax.axis_index("head")
    y, z = seq // NZ, seq % NZ
    me = y * HEADS + head

    def plane_peer(rank):
        return (rank // HEADS * NZ + z, rank % HEADS)

    def line_peer(rank):
        return (y * NZ + rank, head)

    loads = [
        pltpu.make_async_copy(source, target, load_sem.at[index])
        for index, (source, target) in enumerate(
            ((q_ref, qk_in.at[0]), (k_ref, qk_in.at[1]), (v_ref, vg_in.at[0]), (g_ref, vg_in.at[1]))
        )
    ]
    for load in loads:
        load.start()

    barrier = pltpu.get_barrier_semaphore()
    core, x = head % 2, head // 2
    sibling = (seq, head + 1 - 2 * core)

    def greet(peer):
        pl.semaphore_signal(barrier, inc=1, device_id=peer, device_id_type=MESH)

    for i, j in CHIP_STEPS:
        greet(((y + i) % NY * NZ + z, (x + j) % NX * 2))
    greet(sibling)
    for step in LINE_STEPS:
        greet((y * NZ + (z + step) % NZ, 2 * x + 1))

    def met(first):
        @pl.when(core == first)
        def _():
            pl.semaphore_wait(barrier, PLANE - 1)
            pl.semaphore_signal(sync_sem, inc=1, device_id=sibling, device_id_type=MESH)

        @pl.when(core != first)
        def _():
            pl.semaphore_wait(sync_sem, 1)

    met(0)

    def send(source, target, index, peer):
        pltpu.make_async_remote_copy(
            src_ref=source, dst_ref=target, send_sem=send_sem.at[index], recv_sem=recv_sem.at[index],
            device_id=peer, device_id_type=MESH,
        ).start()

    def columns(rank):
        return pl.ds(pl.multiple_of(rank * HD, HD), HD)

    def rows(rank, count):
        return pl.ds(pl.multiple_of(rank * count, count), count)

    def plane_ranks():
        for i, j, k in PLANE_STEPS:
            yield (y + i) % NY * HEADS + (head // 2 + j) % NX * 2 + (head + k) % 2

    def scatter_heads(source, target, index):
        for peer in plane_ranks():
            send(source.at[:, :, columns(peer)], target.at[:, rows(me, ROWS), :], index, plane_peer(peer))

        target[:, rows(me, ROWS), :] = source[:, :, columns(me)]

    def return_to(peer, source, target, index):
        send(source.at[:, rows(peer, ROWS), :], target.at[:, :, columns(me)], index, plane_peer(peer))

    def own_block(source, target, index):
        return pltpu.make_async_copy(
            source.at[:, rows(me, ROWS), :], target.at[:, :, columns(me)], load_sem.at[index]
        )

    def over_line(source, target, index):
        for step in LINE_STEPS:
            peer = (z + step) % NZ
            send(source(peer), target.at[z], index, line_peer(peer))

    def arrived(span, index):
        pltpu.make_async_copy(span, span, recv_sem.at[index]).wait()

    def left(span, index):
        pltpu.make_async_copy(span, span, send_sem.at[index]).wait()

    loads[0].wait()
    loads[1].wait()
    scatter_heads(qk_in, qk, X_QK)
    plane_span = qk.at[:, pl.ds(0, TOK - ROWS), :]
    arrived(plane_span, X_QK)

    for index in range(2):
        summed = jnp.sum(qk[index].astype(F32).reshape(OWN, SEG, HD), axis=1)
        mark_out[index] = (summed * (1.0 / SEG)).astype(BF16)
    met(1)
    over_line(lambda peer: mark_out, marks, X_MARK)
    marks[z] = mark_out[...]
    loads[2].wait()
    loads[3].wait()
    scatter_heads(vg_in, vg, X_VG)
    for index in range(2):
        trans[index] = qk[index].T
    arrived(plane_span, X_VG)
    for index in range(2):
        trans[2 + index] = vg[index].T
    arrived(marks.at[pl.ds(0, NZ - 1)], X_MARK)
    mark_q = marks[:, 0].reshape(M, HD)
    mark_k = marks[:, 1].reshape(M, HD)

    scores = dot_nt(qk[1], mark_q)
    key_top = jnp.max(scores, axis=0, keepdims=True)
    exps = jnp.exp((scores - key_top) * SCALE)
    kexp[...] = exps
    key_sum = jnp.sum(exps, axis=0, keepdims=True)
    stat_out[0:1, :] = key_top
    stat_out[1:2, :] = key_sum
    over_line(lambda peer: stat_out, stats, X_STAT)
    stats[z] = stat_out[...]
    value_part = dot(trans[2], exps.astype(BF16))
    scores = dot_nt(qk[0], mark_k)
    top = jnp.max(scores, axis=1, keepdims=True)
    exps = jnp.exp((scores - top) * SCALE)
    token_prob = exps * (1.0 / jnp.sum(exps, axis=1, keepdims=True))
    prob[...] = token_prob
    token_low = token_prob.astype(BF16)
    low[...] = token_low
    mixing_part = dot(trans[3], token_low)
    pair = [value_part.reshape(NZ, SLAB, M), mixing_part.reshape(NZ, SLAB, M)]
    part_out[...] = jnp.concatenate(pair, axis=1).astype(BF16)
    over_line(lambda peer: part_out.at[peer], parts, X_PART)
    parts[z] = part_out[z]

    scores = dot_nt(mark_q, mark_k)
    exps = jnp.exp((scores - jnp.max(scores, axis=1, keepdims=True)) * SCALE)
    mark_prob = exps * (1.0 / jnp.sum(exps, axis=1, keepdims=True))
    square[0] = mark_prob
    factor = 1.0 / jnp.max(jnp.sum(mark_prob, axis=0, keepdims=True))
    square[1] = mark_prob.T * factor

    def keep(step, slot, value):
        saved[step, slot], saved[step, slot + 1] = split(value)

    def kept(step, slot):
        return saved[step, slot], saved[step, slot + 1]

    keep(ITERS, 8, mark_prob.T)

    @pl.loop(0, ITERS)
    def _(step):
        iterate = square[1]
        keep(step, 0, iterate)
        keep(step, 2, iterate.T)
        part = kept(step, 0)
        product = mul(split(square[0]), part)
        keep(step, 4, product)
        product_split = kept(step, 4)
        first = 7.0 * product - mul(product_split, product_split)
        keep(step, 6, first)
        second = 15.0 * product - mul(product_split, kept(step, 6))
        keep(step, 8, second)
        square[1] = 3.25 * iterate - 0.25 * mul(part, kept(step, 8))

    keep(ITERS, 0, square[1])

    arrived(stats.at[pl.ds(0, NZ - 1)], X_STAT)
    tops = [stats[peer, 0:1, :] for peer in range(NZ)]
    highest = functools.reduce(jnp.maximum, tops)
    weights = [jnp.exp((top - highest) * SCALE) for top in tops]
    total = sum(weight * stats[peer, 1:2, :] for peer, weight in enumerate(weights))
    inverse_total = 1.0 / total
    arrived(parts.at[pl.ds(0, NZ - 1)], X_PART)
    values, mixing_grad = 0.0, 0.0
    for peer in range(NZ):
        part = parts[peer].astype(F32)
        values = values + weights[peer] * part[0:SLAB]
        mixing_grad = mixing_grad + part[SLAB : 2 * SLAB]
    sum_out[...] = jnp.concatenate([values * inverse_total, mixing_grad], axis=0).astype(BF16)
    over_line(lambda peer: sum_out, sums, X_SUM)
    sums[z] = sum_out[...]
    key_prob = kexp[...] * (jnp.exp((key_top - highest) * SCALE) * inverse_total)
    kexp[...] = key_prob
    arrived(sums.at[pl.ds(0, NZ - 1)], X_SUM)
    both = sums[...].astype(F32)
    values = both[:, 0:SLAB, :].reshape(HD, M)
    mixing_grad = both[:, SLAB : 2 * SLAB, :].reshape(HD, M)
    values_split, grad_split = split(values), split(mixing_grad)
    inverse = kept(ITERS, 0)
    mixing_low = mul(values_split, inverse, dot_nt).astype(BF16)
    lv_low = mul(grad_split, inverse).astype(BF16)
    square[1] = mul(split(mixing_grad.T), values_split)
    square[2] = jnp.zeros((M, M), F32)

    token_prob = prob[...]
    av_out[0] = dot_nt(low[...], mixing_low).astype(BF16)
    token_grad = dot(vg[1], mixing_low)
    dots = jnp.sum(token_grad * token_prob, axis=1, keepdims=True)
    token_sgrad = (token_prob * (token_grad - dots)).astype(BF16)
    direct[0] = dot(token_sgrad, mark_k) * SCALE
    grad_out[0] = (dot(trans[0], token_sgrad) * SCALE).T.astype(BF16)
    key_prob = kexp[...]
    av_out[1] = dot_nt(key_prob.astype(BF16), lv_low).astype(BF16)
    row_total = jnp.sum(lv_low.astype(F32) * values, axis=0, keepdims=True)
    key_dgrad = dot(vg[0], lv_low)
    key_sgrad = (key_prob * (key_dgrad - row_total)).astype(BF16)
    direct[1] = dot(key_sgrad, mark_q) * SCALE
    grad_out[1] = (dot(trans[1], key_sgrad) * SCALE).T.astype(BF16)
    over_line(lambda peer: grad_out.at[:, rows(peer, OWN), :], grads, X_GRAD)
    grads[z] = grad_out[:, rows(z, OWN), :]
    own_block(av_out, av_ref, 0).start()
    return_to((me + PLANE - 1) % PLANE, av_out, av_ref, X_AV)

    square[3] = -0.25 * mul(kept(ITERS - 1, 2), split(square[1]))

    def step_back(step, before):
        second_grad = square[3]
        second_split = split(second_grad)
        product_split = kept(step, 4)
        first_split = kept(step, 6)
        through = split(mul(product_split, second_split))
        product_grad = 15.0 * second_grad - (mul(second_split, first_split) + mul(first_split, second_split))
        product_grad = split(product_grad + mul(through, product_split))
        out_grad = square[1]
        out_grad = 3.25 * out_grad - 0.25 * mul(split(out_grad), kept(step, 8))
        earlier = mul(kept(before, 2), split(out_grad))
        square[3] = -0.25 * (earlier + mul(kept(before, 4), product_grad))
        square[1] = out_grad + mul(kept(ITERS, 8), product_grad)
        square[2] += mul(product_grad, kept(step, 0), dot_nt)

    step_back(ITERS - 1, ITERS - 2)

    @pl.loop(1, ITERS)
    def _(back):
        for turn in range(6):
            return_to((me + 1 + (back - 1) * 6 + turn) % PLANE, av_out, av_ref, X_AV)
        step = ITERS - 1 - back
        step_back(step, jnp.maximum(step - 1, 0))

    mark_grad = square[2] + square[1].T * factor
    mark_prob = square[0]
    mark_sgrad = mark_prob * (mark_grad - jnp.sum(mark_grad * mark_prob, axis=1, keepdims=True))
    square[1] = mark_sgrad
    square[2] = mark_sgrad.T
    arrived(grads.at[pl.ds(0, NZ - 1)], X_GRAD)
    from_query, from_key = split(square[1, rows(z, OWN), :]), split(square[2, rows(z, OWN), :])
    query_marks = (dot(from_query[0], mark_k) + dot(from_query[1], mark_k)) * SCALE
    key_marks = (dot(from_key[0], mark_q) + dot(from_key[1], mark_q)) * SCALE
    for peer in range(NZ):
        query_marks = query_marks + grads[peer, 1].astype(F32)
        key_marks = key_marks + grads[peer, 0].astype(F32)
    for index, total in ((0, query_marks), (1, key_marks)):
        spread = direct[index].reshape(OWN, SEG, HD) + (total * (1.0 / SEG))[:, None, :]
        qk_out[index] = spread.reshape(TOK, HD).astype(BF16)
    for peer in plane_ranks():
        return_to(peer, qk_out, qk_ref, X_OUT)
    own_block(qk_out, qk_ref, 1).start()

    out_span = av_ref.at[:, :, pl.ds(0, D - HD)]
    own_block(av_out, av_ref, 0).wait()
    own_block(qk_out, qk_ref, 1).wait()
    arrived(out_span, X_AV)
    arrived(out_span, X_OUT)
    for index in (X_QK, X_VG, X_AV, X_OUT):
        left(plane_span, index)
    left(marks.at[pl.ds(0, NZ - 1)], X_MARK)
    left(stats.at[pl.ds(0, NZ - 1)], X_STAT); left(parts.at[pl.ds(0, NZ - 1)], X_PART)
    left(sums.at[pl.ds(0, NZ - 1)], X_SUM)
    left(grads.at[pl.ds(0, NZ - 1)], X_GRAD)


def body(queries, keys, values, out_grad):
    pair = jax.ShapeDtypeStruct((2, ROWS, D), BF16)
    anywhere = pl.BlockSpec(memory_space=pl.ANY)
    av, qk = pl.pallas_call(
        kernel,
        out_shape=(pair, pair),
        in_specs=[anywhere] * 4,
        out_specs=(anywhere, anywhere),
        scratch_shapes=[
            pltpu.VMEM((2, ROWS, D), BF16),
            pltpu.VMEM((2, ROWS, D), BF16),
            pltpu.VMEM((2, TOK, HD), BF16),
            pltpu.VMEM((2, TOK, HD), BF16),
            pltpu.VMEM((2, OWN, HD), BF16),
            pltpu.VMEM((NZ, 2, OWN, HD), BF16),
            pltpu.VMEM((NZ, 2 * SLAB, M), BF16),
            pltpu.VMEM((NZ, 2 * SLAB, M), BF16),
            pltpu.VMEM((2, M), F32),
            pltpu.VMEM((NZ, 2, M), F32),
            pltpu.VMEM((2 * SLAB, M), BF16),
            pltpu.VMEM((NZ, 2 * SLAB, M), BF16),
            pltpu.VMEM((2, TOK, HD), BF16),
            pltpu.VMEM((2, M, HD), BF16),
            pltpu.VMEM((NZ, 2, OWN, HD), BF16),
            pltpu.VMEM((2, TOK, HD), BF16),
            pltpu.VMEM((TOK, M), F32),
            pltpu.VMEM((TOK, M), BF16),
            pltpu.VMEM((TOK, M), F32),
            pltpu.VMEM((4, HD, TOK), BF16),
            pltpu.VMEM((2, TOK, HD), F32),
            pltpu.VMEM((4, M, M), F32),
            pltpu.VMEM((ITERS + 1, 10, M, M), BF16),
            pltpu.SemaphoreType.REGULAR,
            pltpu.SemaphoreType.DMA((4,)),
            pltpu.SemaphoreType.DMA((9,)),
            pltpu.SemaphoreType.DMA((9,)),
        ],
        compiler_params=pltpu.CompilerParams(
            collective_id=0, has_side_effects=True, vmem_limit_bytes=63 * 1024 * 1024
        ),
    )(queries, keys, values, out_grad)
    return av[0], qk[0], qk[1], av[1]


def solution(mesh):
    spec = P(("seq", "head"), None)
    return jax.shard_map(body, mesh=mesh, in_specs=(spec,) * 4, out_specs=(spec,) * 4, check_vma=False)
```

```python
import functools

import jax
import jax.numpy as jnp
from jax import lax
from jax.experimental import pallas as pl
from jax.experimental.pallas import tpu as pltpu
from jax.sharding import PartitionSpec as P

MESH = pl.DeviceIdType.MESH
F32, BF16 = jnp.float32, jnp.bfloat16

NZ = 16
PLANE = 32
HEADS = 8
ROWS = 16
HD = 128
D = PLANE * HD
TOK = PLANE * ROWS
SEG = 32
OWN = TOK // SEG
M = NZ * OWN
SLAB = HD // NZ
ITERS = 6
SCALE = HD ** (-0.5)


def away(step, size):
    return min(step % size, -step % size)


NY, NX = 4, 4
PLANE_STEPS = sorted(
    ((i, j, k) for i in range(NY) for j in range(NX) for k in range(2) if i or j or k),
    key=lambda step: -away(step[0], NY) - away(step[1], NX),
)
CHIP_STEPS = [(i, j) for i, j, k in PLANE_STEPS if k == 0]
LINE_STEPS = sorted(range(1, NZ), key=lambda step: -away(step, NZ))

X_QK, X_VG, X_MARK, X_PART, X_SUM, X_AV, X_GRAD, X_OUT, X_STAT = range(9)


def dot(left, right):
    return lax.dot_general(left, right, (((1,), (0,)), ((), ())), preferred_element_type=F32)


def dot_nt(left, right):
    return lax.dot_general(left, right, (((1,), (1,)), ((), ())), preferred_element_type=F32)


def split(x):
    high = x.astype(BF16)
    return high, (x - high.astype(F32)).astype(BF16)


def mul(left, right, product=dot):
    return product(left[0], right[0]) + (product(left[0], right[1]) + product(left[1], right[0]))


def mul_left(left, right, product=dot):
    return product(left, right[0]) + product(left, right[1])


def mul_right(left, right):
    return dot(left[0], right) + dot(left[1], right)


def kernel(
    q_ref, k_ref, v_ref, g_ref, av_ref, qk_ref,
    qk_in, vg_in, qk, vg, mark_out, marks, part_out, parts, stat_out, stats, sum_out, sums, av_out, grad_out, grads, qk_out,
    prob, low, kexp, trans, direct, square, saved, sync_sem, load_sem, send_sem, recv_sem,
):
    seq, head = lax.axis_index("seq"), lax.axis_index("head")
    y, z = seq // NZ, seq % NZ
    me = y * HEADS + head

    def plane_peer(rank):
        return (rank // HEADS * NZ + z, rank % HEADS)

    def line_peer(rank):
        return (y * NZ + rank, head)

    loads = [
        pltpu.make_async_copy(source, target, load_sem.at[index])
        for index, (source, target) in enumerate(
            ((q_ref, qk_in.at[0]), (k_ref, qk_in.at[1]), (v_ref, vg_in.at[0]), (g_ref, vg_in.at[1]))
        )
    ]
    for load in loads:
        load.start()

    barrier = pltpu.get_barrier_semaphore()
    core, x = head % 2, head // 2
    sibling = (seq, head + 1 - 2 * core)

    def greet(peer):
        pl.semaphore_signal(barrier, inc=1, device_id=peer, device_id_type=MESH)

    for i, j in CHIP_STEPS:
        greet(((y + i) % NY * NZ + z, (x + j) % NX * 2))
    greet(sibling)
    for step in LINE_STEPS:
        greet((y * NZ + (z + step) % NZ, 2 * x + 1))

    def met(first):
        @pl.when(core == first)
        def _():
            pl.semaphore_wait(barrier, PLANE - 1)
            pl.semaphore_signal(sync_sem, inc=1, device_id=sibling, device_id_type=MESH)

        @pl.when(core != first)
        def _():
            pl.semaphore_wait(sync_sem, 1)

    met(0)

    def send(source, target, index, peer):
        pltpu.make_async_remote_copy(
            src_ref=source, dst_ref=target, send_sem=send_sem.at[index], recv_sem=recv_sem.at[index],
            device_id=peer, device_id_type=MESH,
        ).start()

    def columns(rank):
        return pl.ds(pl.multiple_of(rank * HD, HD), HD)

    def rows(rank, count):
        return pl.ds(pl.multiple_of(rank * count, count), count)

    def plane_ranks():
        for i, j, k in PLANE_STEPS:
            yield (y + i) % NY * HEADS + (head // 2 + j) % NX * 2 + (head + k) % 2

    def scatter_heads(source, target, index):
        for peer in plane_ranks():
            send(source.at[:, :, columns(peer)], target.at[:, rows(me, ROWS), :], index, plane_peer(peer))

        target[:, rows(me, ROWS), :] = source[:, :, columns(me)]

    def return_to(peer, source, target, index):
        send(source.at[:, rows(peer, ROWS), :], target.at[:, :, columns(me)], index, plane_peer(peer))

    def own_block(source, target, index):
        return pltpu.make_async_copy(
            source.at[:, rows(me, ROWS), :], target.at[:, :, columns(me)], load_sem.at[index]
        )

    def over_line(source, target, index):
        for step in LINE_STEPS:
            peer = (z + step) % NZ
            send(source(peer), target.at[z], index, line_peer(peer))

    def arrived(span, index):
        pltpu.make_async_copy(span, span, recv_sem.at[index]).wait()

    def left(span, index):
        pltpu.make_async_copy(span, span, send_sem.at[index]).wait()

    loads[0].wait()
    loads[1].wait()
    scatter_heads(qk_in, qk, X_QK)
    plane_span = qk.at[:, pl.ds(0, TOK - ROWS), :]
    arrived(plane_span, X_QK)

    for index in range(2):
        summed = jnp.sum(qk[index].astype(F32).reshape(OWN, SEG, HD), axis=1)
        mark_out[index] = (summed * (1.0 / SEG)).astype(BF16)
    met(1)
    over_line(lambda peer: mark_out, marks, X_MARK)
    marks[z] = mark_out[...]
    loads[2].wait()
    loads[3].wait()
    scatter_heads(vg_in, vg, X_VG)
    for index in range(2):
        trans[index] = qk[index].T
    arrived(marks.at[pl.ds(0, NZ - 1)], X_MARK)
    mark_q = marks[:, 0].reshape(M, HD)
    mark_k = marks[:, 1].reshape(M, HD)

    scores = dot_nt(qk[1], mark_q)
    key_top = jnp.max(scores, axis=0, keepdims=True)
    exps = jnp.exp((scores - key_top) * SCALE)
    kexp[...] = exps
    key_sum = jnp.sum(exps, axis=0, keepdims=True)
    stat_out[0:1, :] = key_top
    stat_out[1:2, :] = key_sum
    over_line(lambda peer: stat_out, stats, X_STAT)
    stats[z] = stat_out[...]
    arrived(plane_span, X_VG)
    for index in range(2):
        trans[2 + index] = vg[index].T
    value_part = dot(trans[2], exps.astype(BF16))
    scores = dot_nt(qk[0], mark_k)
    top = jnp.max(scores, axis=1, keepdims=True)
    exps = jnp.exp((scores - top) * SCALE)
    token_prob = exps * (1.0 / jnp.sum(exps, axis=1, keepdims=True))
    prob[...] = token_prob
    token_low = token_prob.astype(BF16)
    low[...] = token_low
    mixing_part = dot(trans[3], token_low)
    pair = [value_part.reshape(NZ, SLAB, M), mixing_part.reshape(NZ, SLAB, M)]
    part_out[...] = jnp.concatenate(pair, axis=1).astype(BF16)
    over_line(lambda peer: part_out.at[peer], parts, X_PART)
    parts[z] = part_out[z]

    scores = dot_nt(mark_q, mark_k)
    exps = jnp.exp((scores - jnp.max(scores, axis=1, keepdims=True)) * SCALE)
    mark_prob = exps * (1.0 / jnp.sum(exps, axis=1, keepdims=True))
    square[0] = mark_prob
    factor = 1.0 / jnp.max(jnp.sum(mark_prob, axis=0, keepdims=True))
    square[1] = mark_prob.T * factor

    def keep(step, slot, value):
        saved[step, slot], saved[step, slot + 1] = split(value)

    def kept(step, slot):
        return saved[step, slot], saved[step, slot + 1]

    keep(ITERS, 8, mark_prob.T)

    @pl.loop(0, ITERS)
    def _(step):
        iterate = square[1]
        keep(step, 0, iterate)
        keep(step, 2, iterate.T)
        part = kept(step, 0)
        product = mul(split(square[0]), part)
        keep(step, 4, product)
        product_split = kept(step, 4)
        first = 7.0 * product - mul(product_split, product_split)
        keep(step, 6, first)
        second = 15.0 * product - mul(product_split, kept(step, 6))
        keep(step, 8, second)
        square[1] = 3.25 * iterate - 0.25 * mul(part, kept(step, 8))

    keep(ITERS, 0, square[1])

    arrived(stats.at[pl.ds(0, NZ - 1)], X_STAT)
    tops = [stats[peer, 0:1, :] for peer in range(NZ)]
    highest = functools.reduce(jnp.maximum, tops)
    weights = [jnp.exp((top - highest) * SCALE) for top in tops]
    total = sum(weight * stats[peer, 1:2, :] for peer, weight in enumerate(weights))
    inverse_total = 1.0 / total
    arrived(parts.at[pl.ds(0, NZ - 1)], X_PART)
    values, mixing_grad = 0.0, 0.0
    for peer in range(NZ):
        part = parts[peer].astype(F32)
        values = values + weights[peer] * part[0:SLAB]
        mixing_grad = mixing_grad + part[SLAB : 2 * SLAB]
    sum_out[...] = jnp.concatenate([values * inverse_total, mixing_grad], axis=0).astype(BF16)
    over_line(lambda peer: sum_out, sums, X_SUM)
    sums[z] = sum_out[...]
    key_prob = kexp[...] * (jnp.exp((key_top - highest) * SCALE) * inverse_total)
    kexp[...] = key_prob
    arrived(sums.at[pl.ds(0, NZ - 1)], X_SUM)
    both = sums[...].astype(F32)
    values = both[:, 0:SLAB, :].reshape(HD, M)
    values_low, mixing_grad = values.astype(BF16), both[:, SLAB : 2 * SLAB, :].reshape(HD, M).astype(BF16)
    inverse = kept(ITERS, 0)
    square[1] = dot(mixing_grad.T, values_low)
    mixing_low = (mul_left(values_low, inverse, dot_nt)).astype(BF16)
    lv_low = (mul_left(mixing_grad, inverse)).astype(BF16)
    square[2] = jnp.zeros((M, M), F32)

    token_prob = prob[...]
    av_out[0] = dot_nt(low[...], mixing_low).astype(BF16)
    token_grad = dot(vg[1], mixing_low)
    dots = jnp.sum(token_grad * token_prob, axis=1, keepdims=True)
    token_sgrad = (token_prob * (token_grad - dots)).astype(BF16)
    direct[0] = dot(token_sgrad, mark_k) * SCALE
    grad_out[0] = (dot(trans[0], token_sgrad) * SCALE).T.astype(BF16)
    key_prob = kexp[...]
    av_out[1] = dot_nt(key_prob.astype(BF16), lv_low).astype(BF16)
    row_total = jnp.sum(lv_low.astype(F32) * values, axis=0, keepdims=True)
    key_dgrad = dot(vg[0], lv_low)
    key_sgrad = (key_prob * (key_dgrad - row_total)).astype(BF16)
    direct[1] = dot(key_sgrad, mark_q) * SCALE
    grad_out[1] = (dot(trans[1], key_sgrad) * SCALE).T.astype(BF16)
    over_line(lambda peer: grad_out.at[:, rows(peer, OWN), :], grads, X_GRAD)
    grads[z] = grad_out[:, rows(z, OWN), :]
    own_block(av_out, av_ref, 0).start()

    square[3] = -0.25 * mul_right(kept(ITERS - 1, 2), square[1].astype(BF16))

    def step_back(step, before):
        second_grad = square[3]
        second_low = second_grad.astype(BF16)
        product_split = kept(step, 4)
        first_split = kept(step, 6)
        through = mul_right(product_split, second_low).astype(BF16)
        product_grad = 15.0 * second_grad - (mul_left(second_low, first_split) + mul_right(first_split, second_low))
        product_grad = (product_grad + mul_left(through, product_split)).astype(BF16)
        out_grad = square[1]
        out_grad = 3.25 * out_grad - 0.25 * mul_left(out_grad.astype(BF16), kept(step, 8))
        if before is not None:
            earlier = mul_right(kept(before, 2), out_grad.astype(BF16))
            square[3] = -0.25 * (earlier + mul_right(kept(before, 4), product_grad))
        square[1] = out_grad + mul_right(kept(ITERS, 8), product_grad)
        square[2] += mul_left(product_grad, kept(step, 0), dot_nt)

    step_back(ITERS - 1, ITERS - 2)
    for turn in range(3):
        return_to((me + 1 + turn) % PLANE, av_out, av_ref, X_AV)

    @pl.loop(1, ITERS - 1)
    def _(back):
        for turn in range(7):
            return_to((me + 4 + (back - 1) * 7 + turn) % PLANE, av_out, av_ref, X_AV)
        step_back(ITERS - 1 - back, ITERS - 2 - back)

    step_back(0, None)

    mark_grad = square[2] + square[1].T * factor
    mark_prob = square[0]
    mark_sgrad = mark_prob * (mark_grad - jnp.sum(mark_grad * mark_prob, axis=1, keepdims=True))
    square[1] = mark_sgrad
    square[2] = mark_sgrad.T
    arrived(grads.at[pl.ds(0, NZ - 1)], X_GRAD)
    from_query, from_key = split(square[1, rows(z, OWN), :]), split(square[2, rows(z, OWN), :])
    query_marks = (dot(from_query[0], mark_k) + dot(from_query[1], mark_k)) * SCALE
    key_marks = (dot(from_key[0], mark_q) + dot(from_key[1], mark_q)) * SCALE
    for peer in range(NZ):
        query_marks = query_marks + grads[peer, 1].astype(F32)
        key_marks = key_marks + grads[peer, 0].astype(F32)
    for index, total in ((0, query_marks), (1, key_marks)):
        spread = direct[index].reshape(OWN, SEG, HD) + (total * (1.0 / SEG))[:, None, :]
        qk_out[index] = spread.reshape(TOK, HD).astype(BF16)
    for peer in plane_ranks():
        return_to(peer, qk_out, qk_ref, X_OUT)
    own_block(qk_out, qk_ref, 1).start()

    out_span = av_ref.at[:, :, pl.ds(0, D - HD)]
    own_block(av_out, av_ref, 0).wait()
    own_block(qk_out, qk_ref, 1).wait()
    arrived(out_span, X_AV)
    arrived(out_span, X_OUT)
    for index in (X_QK, X_VG, X_AV, X_OUT):
        left(plane_span, index)
    left(marks.at[pl.ds(0, NZ - 1)], X_MARK)
    left(stats.at[pl.ds(0, NZ - 1)], X_STAT); left(parts.at[pl.ds(0, NZ - 1)], X_PART)
    left(sums.at[pl.ds(0, NZ - 1)], X_SUM)
    left(grads.at[pl.ds(0, NZ - 1)], X_GRAD)


def body(queries, keys, values, out_grad):
    pair = jax.ShapeDtypeStruct((2, ROWS, D), BF16)
    anywhere = pl.BlockSpec(memory_space=pl.ANY)
    av, qk = pl.pallas_call(
        kernel,
        out_shape=(pair, pair),
        in_specs=[anywhere] * 4,
        out_specs=(anywhere, anywhere),
        scratch_shapes=[
            pltpu.VMEM((2, ROWS, D), BF16),
            pltpu.VMEM((2, ROWS, D), BF16),
            pltpu.VMEM((2, TOK, HD), BF16),
            pltpu.VMEM((2, TOK, HD), BF16),
            pltpu.VMEM((2, OWN, HD), BF16),
            pltpu.VMEM((NZ, 2, OWN, HD), BF16),
            pltpu.VMEM((NZ, 2 * SLAB, M), BF16),
            pltpu.VMEM((NZ, 2 * SLAB, M), BF16),
            pltpu.VMEM((2, M), F32),
            pltpu.VMEM((NZ, 2, M), F32),
            pltpu.VMEM((2 * SLAB, M), BF16),
            pltpu.VMEM((NZ, 2 * SLAB, M), BF16),
            pltpu.VMEM((2, TOK, HD), BF16),
            pltpu.VMEM((2, M, HD), BF16),
            pltpu.VMEM((NZ, 2, OWN, HD), BF16),
            pltpu.VMEM((2, TOK, HD), BF16),
            pltpu.VMEM((TOK, M), F32),
            pltpu.VMEM((TOK, M), BF16),
            pltpu.VMEM((TOK, M), F32),
            pltpu.VMEM((4, HD, TOK), BF16),
            pltpu.VMEM((2, TOK, HD), F32),
            pltpu.VMEM((4, M, M), F32),
            pltpu.VMEM((ITERS + 1, 10, M, M), BF16),
            pltpu.SemaphoreType.REGULAR,
            pltpu.SemaphoreType.DMA((4,)),
            pltpu.SemaphoreType.DMA((9,)),
            pltpu.SemaphoreType.DMA((9,)),
        ],
        compiler_params=pltpu.CompilerParams(
            collective_id=0, has_side_effects=True, vmem_limit_bytes=63 * 1024 * 1024
        ),
    )(queries, keys, values, out_grad)
    return av[0], qk[0], qk[1], av[1]


def solution(mesh):
    spec = P(("seq", "head"), None)
    return jax.shard_map(body, mesh=mesh, in_specs=(spec,) * 4, out_specs=(spec,) * 4, check_vma=False)
```

```python
import functools

import jax
import jax.numpy as jnp
from jax import lax
from jax.experimental import pallas as pl
from jax.experimental.pallas import tpu as pltpu
from jax.sharding import PartitionSpec as P

MESH = pl.DeviceIdType.MESH
F32, BF16 = jnp.float32, jnp.bfloat16

NZ = 16
PLANE = 32
HEADS = 8
ROWS = 16
HD = 128
D = PLANE * HD
TOK = PLANE * ROWS
SEG = 32
OWN = TOK // SEG
M = NZ * OWN
SLAB = HD // NZ
ITERS = 6
SCALE = HD ** (-0.5)


def away(step, size):
    return min(step % size, -step % size)


NY, NX = 4, 4
PLANE_STEPS = sorted(
    ((i, j, k) for i in range(NY) for j in range(NX) for k in range(2) if i or j or k),
    key=lambda step: -away(step[0], NY) - away(step[1], NX),
)
CHIP_STEPS = [(i, j) for i, j, k in PLANE_STEPS if k == 0]
LINE_STEPS = sorted(range(1, NZ), key=lambda step: -away(step, NZ))

X_QK, X_VG, X_MARK, X_PART, X_SUM, X_AV, X_GRAD, X_OUT, X_STAT, X_GRAD_B = range(10)


def dot(left, right):
    return lax.dot_general(left, right, (((1,), (0,)), ((), ())), preferred_element_type=F32)


def dot_nt(left, right):
    return lax.dot_general(left, right, (((1,), (1,)), ((), ())), preferred_element_type=F32)


def split(x):
    high = x.astype(BF16)
    return high, (x - high.astype(F32)).astype(BF16)


def mul(left, right, product=dot):
    return product(left[0], right[0]) + (product(left[0], right[1]) + product(left[1], right[0]))


def mul_left(left, right, product=dot):
    return product(left, right[0]) + product(left, right[1])


def mul_right(left, right):
    return dot(left[0], right) + dot(left[1], right)


def kernel(
    q_ref, k_ref, v_ref, g_ref, av_ref, qk_ref,
    qk_in, vg_in, qk, vg, mark_out, marks, part_out, parts, stat_out, stats, sum_out, sums, av_out, grad_out, grads, qk_out,
    prob, low, kexp, trans, direct, square, saved, sync_sem, load_sem, send_sem, recv_sem,
):
    seq, head = lax.axis_index("seq"), lax.axis_index("head")
    y, z = seq // NZ, seq % NZ
    me = y * HEADS + head

    def plane_peer(rank):
        return (rank // HEADS * NZ + z, rank % HEADS)

    def line_peer(rank):
        return (y * NZ + rank, head)

    loads = [
        pltpu.make_async_copy(source, target, load_sem.at[index])
        for index, (source, target) in enumerate(
            ((q_ref, qk_in.at[0]), (k_ref, qk_in.at[1]), (v_ref, vg_in.at[0]), (g_ref, vg_in.at[1]))
        )
    ]
    for load in loads:
        load.start()

    barrier = pltpu.get_barrier_semaphore()
    core, x = head % 2, head // 2
    sibling = (seq, head + 1 - 2 * core)

    def greet(peer):
        pl.semaphore_signal(barrier, inc=1, device_id=peer, device_id_type=MESH)

    for i, j in CHIP_STEPS:
        greet(((y + i) % NY * NZ + z, (x + j) % NX * 2))
    greet(sibling)
    for step in LINE_STEPS:
        greet((y * NZ + (z + step) % NZ, 2 * x + 1))

    def met(first):
        @pl.when(core == first)
        def _():
            pl.semaphore_wait(barrier, PLANE - 1)
            pl.semaphore_signal(sync_sem, inc=1, device_id=sibling, device_id_type=MESH)

        @pl.when(core != first)
        def _():
            pl.semaphore_wait(sync_sem, 1)

    met(0)

    def send(source, target, index, peer):
        pltpu.make_async_remote_copy(
            src_ref=source, dst_ref=target, send_sem=send_sem.at[index], recv_sem=recv_sem.at[index],
            device_id=peer, device_id_type=MESH,
        ).start()

    def columns(rank):
        return pl.ds(pl.multiple_of(rank * HD, HD), HD)

    def rows(rank, count):
        return pl.ds(pl.multiple_of(rank * count, count), count)

    def plane_ranks():
        for i, j, k in PLANE_STEPS:
            yield (y + i) % NY * HEADS + (head // 2 + j) % NX * 2 + (head + k) % 2

    def scatter_heads(source, target, index):
        for peer in plane_ranks():
            send(source.at[:, :, columns(peer)], target.at[:, rows(me, ROWS), :], index, plane_peer(peer))

        target[:, rows(me, ROWS), :] = source[:, :, columns(me)]

    def return_to(peer, source, target, index):
        send(source.at[:, rows(peer, ROWS), :], target.at[:, :, columns(me)], index, plane_peer(peer))

    def own_block(source, target, index):
        return pltpu.make_async_copy(
            source.at[:, rows(me, ROWS), :], target.at[:, :, columns(me)], load_sem.at[index]
        )

    def over_line(source, target, index):
        for step in LINE_STEPS:
            peer = (z + step) % NZ
            send(source(peer), target.at[z], index, line_peer(peer))

    def arrived(span, index):
        pltpu.make_async_copy(span, span, recv_sem.at[index]).wait()

    def left(span, index):
        pltpu.make_async_copy(span, span, send_sem.at[index]).wait()

    loads[0].wait()
    loads[1].wait()
    scatter_heads(qk_in, qk, X_QK)
    plane_span = qk.at[:, pl.ds(0, TOK - ROWS), :]
    arrived(plane_span, X_QK)

    for index in range(2):
        summed = jnp.sum(qk[index].astype(F32).reshape(OWN, SEG, HD), axis=1)
        mark_out[index] = (summed * (1.0 / SEG)).astype(BF16)
    met(1)
    over_line(lambda peer: mark_out, marks, X_MARK)
    marks[z] = mark_out[...]
    loads[2].wait()
    loads[3].wait()
    scatter_heads(vg_in, vg, X_VG)
    for index in range(2):
        trans[index] = qk[index].T
    arrived(marks.at[pl.ds(0, NZ - 1)], X_MARK)
    mark_q = marks[:, 0].reshape(M, HD)
    mark_k = marks[:, 1].reshape(M, HD)

    scores = dot_nt(qk[1], mark_q)
    key_top = jnp.max(scores, axis=0, keepdims=True)
    exps = jnp.exp((scores - key_top) * SCALE)
    kexp[...] = exps
    key_sum = jnp.sum(exps, axis=0, keepdims=True)
    stat_out[0:1, :] = key_top
    stat_out[1:2, :] = key_sum
    over_line(lambda peer: stat_out, stats, X_STAT)
    stats[z] = stat_out[...]
    arrived(plane_span, X_VG)
    for index in range(2):
        trans[2 + index] = vg[index].T
    value_part = dot(trans[2], exps.astype(BF16))
    scores = dot_nt(qk[0], mark_k)
    top = jnp.max(scores, axis=1, keepdims=True)
    exps = jnp.exp((scores - top) * SCALE)
    token_prob = exps * (1.0 / jnp.sum(exps, axis=1, keepdims=True))
    prob[...] = token_prob
    token_low = token_prob.astype(BF16)
    low[...] = token_low
    mixing_part = dot(trans[3], token_low)
    pair = [value_part.reshape(NZ, SLAB, M), mixing_part.reshape(NZ, SLAB, M)]
    part_out[...] = jnp.concatenate(pair, axis=1).astype(BF16)
    over_line(lambda peer: part_out.at[peer], parts, X_PART)
    parts[z] = part_out[z]

    scores = dot_nt(mark_q, mark_k)
    exps = jnp.exp((scores - jnp.max(scores, axis=1, keepdims=True)) * SCALE)
    mark_prob = exps * (1.0 / jnp.sum(exps, axis=1, keepdims=True))
    square[0] = mark_prob
    factor = 1.0 / jnp.max(jnp.sum(mark_prob, axis=0, keepdims=True))
    square[1] = mark_prob.T * factor

    def keep(step, slot, value):
        saved[step, slot], saved[step, slot + 1] = split(value)

    def kept(step, slot):
        return saved[step, slot], saved[step, slot + 1]

    keep(ITERS, 8, mark_prob.T)

    @pl.loop(0, ITERS)
    def _(step):
        iterate = square[1]
        keep(step, 0, iterate)
        keep(step, 2, iterate.T)
        part = kept(step, 0)
        product = mul(split(square[0]), part)
        keep(step, 4, product)
        product_split = kept(step, 4)
        first = 7.0 * product - mul(product_split, product_split)
        keep(step, 6, first)
        second = 15.0 * product - mul(product_split, kept(step, 6))
        keep(step, 8, second)
        square[1] = 3.25 * iterate - 0.25 * mul(part, kept(step, 8))

    keep(ITERS, 0, square[1])

    arrived(stats.at[pl.ds(0, NZ - 1)], X_STAT)
    tops = [stats[peer, 0:1, :] for peer in range(NZ)]
    highest = functools.reduce(jnp.maximum, tops)
    weights = [jnp.exp((top - highest) * SCALE) for top in tops]
    total = sum(weight * stats[peer, 1:2, :] for peer, weight in enumerate(weights))
    inverse_total = 1.0 / total
    arrived(parts.at[pl.ds(0, NZ - 1)], X_PART)
    values, mixing_grad = 0.0, 0.0
    for peer in range(NZ):
        part = parts[peer].astype(F32)
        values = values + weights[peer] * part[0:SLAB]
        mixing_grad = mixing_grad + part[SLAB : 2 * SLAB]
    sum_out[...] = jnp.concatenate([values * inverse_total, mixing_grad], axis=0).astype(BF16)
    over_line(lambda peer: sum_out, sums, X_SUM)
    sums[z] = sum_out[...]
    key_prob = kexp[...] * (jnp.exp((key_top - highest) * SCALE) * inverse_total)
    kexp[...] = key_prob
    arrived(sums.at[pl.ds(0, NZ - 1)], X_SUM)
    both = sums[...].astype(F32)
    values = both[:, 0:SLAB, :].reshape(HD, M)
    values_low, mixing_grad = values.astype(BF16), both[:, SLAB : 2 * SLAB, :].reshape(HD, M).astype(BF16)
    inverse = kept(ITERS, 0)
    square[1] = dot(mixing_grad.T, values_low)
    mixing_low = (mul_left(values_low, inverse, dot_nt)).astype(BF16)
    lv_low = (mul_left(mixing_grad, inverse)).astype(BF16)
    square[2] = jnp.zeros((M, M), F32)

    token_prob = prob[...]
    av_out[0] = dot_nt(low[...], mixing_low).astype(BF16)
    token_grad = dot(vg[1], mixing_low)
    dots = jnp.sum(token_grad * token_prob, axis=1, keepdims=True)
    token_sgrad = (token_prob * (token_grad - dots)).astype(BF16)
    direct[0] = dot(token_sgrad, mark_k) * SCALE
    grad_out[0] = (dot(trans[0], token_sgrad) * SCALE).astype(BF16).T
    over_line(lambda peer: grad_out.at[0, rows(peer, OWN), :], grads.at[0], X_GRAD)
    key_prob = kexp[...]
    av_out[1] = dot_nt(key_prob.astype(BF16), lv_low).astype(BF16)
    row_total = jnp.sum(lv_low.astype(F32) * values, axis=0, keepdims=True)
    key_dgrad = dot(vg[0], lv_low)
    key_sgrad = (key_prob * (key_dgrad - row_total)).astype(BF16)
    direct[1] = dot(key_sgrad, mark_q) * SCALE
    grad_out[1] = (dot(trans[1], key_sgrad) * SCALE).astype(BF16).T
    over_line(lambda peer: grad_out.at[1, rows(peer, OWN), :], grads.at[1], X_GRAD_B)
    for index in range(2):
        grads[index, z] = grad_out[index, rows(z, OWN), :]
    own_block(av_out, av_ref, 0).start()

    square[3] = -0.25 * mul_right(kept(ITERS - 1, 2), square[1].astype(BF16))

    def step_back(step, before):
        second_grad = square[3]
        second_low = second_grad.astype(BF16)
        product_split = kept(step, 4)
        first_split = kept(step, 6)
        through = mul_right(product_split, second_low).astype(BF16)
        product_grad = 15.0 * second_grad - (mul_left(second_low, first_split) + mul_right(first_split, second_low))
        product_grad = (product_grad + mul_left(through, product_split)).astype(BF16)
        out_grad = square[1]
        out_grad = 3.25 * out_grad - 0.25 * mul_left(out_grad.astype(BF16), kept(step, 8))
        if before is not None:
            earlier = mul_right(kept(before, 2), out_grad.astype(BF16))
            square[3] = -0.25 * (earlier + mul_right(kept(before, 4), product_grad))
        square[1] = out_grad + mul_right(kept(ITERS, 8), product_grad)
        square[2] += mul_left(product_grad, kept(step, 0), dot_nt)

    step_back(ITERS - 1, ITERS - 2)
    for turn in range(3):
        return_to((me + 1 + turn) % PLANE, av_out, av_ref, X_AV)

    @pl.loop(1, ITERS - 1)
    def _(back):
        for turn in range(7):
            return_to((me + 4 + (back - 1) * 7 + turn) % PLANE, av_out, av_ref, X_AV)
        step_back(ITERS - 1 - back, ITERS - 2 - back)

    step_back(0, None)

    mark_grad = square[2] + square[1].T * factor
    mark_prob = square[0]
    mark_sgrad = mark_prob * (mark_grad - jnp.sum(mark_grad * mark_prob, axis=1, keepdims=True))
    square[1] = mark_sgrad
    square[2] = mark_sgrad.T
    grad_span = grads.at[0, pl.ds(0, NZ - 1)]
    arrived(grad_span, X_GRAD)
    arrived(grad_span, X_GRAD_B)
    from_query, from_key = split(square[1, rows(z, OWN), :]), split(square[2, rows(z, OWN), :])
    query_marks = (dot(from_query[0], mark_k) + dot(from_query[1], mark_k)) * SCALE
    key_marks = (dot(from_key[0], mark_q) + dot(from_key[1], mark_q)) * SCALE
    for peer in range(NZ):
        query_marks = query_marks + grads[1, peer].astype(F32)
        key_marks = key_marks + grads[0, peer].astype(F32)
    for index, total in ((0, query_marks), (1, key_marks)):
        spread = direct[index].reshape(OWN, SEG, HD) + (total * (1.0 / SEG))[:, None, :]
        qk_out[index] = spread.reshape(TOK, HD).astype(BF16)
    for peer in plane_ranks():
        return_to(peer, qk_out, qk_ref, X_OUT)
    own_block(qk_out, qk_ref, 1).start()

    out_span = av_ref.at[:, :, pl.ds(0, D - HD)]
    own_block(av_out, av_ref, 0).wait()
    own_block(qk_out, qk_ref, 1).wait()
    arrived(out_span, X_AV)
    arrived(out_span, X_OUT)
    for index in (X_QK, X_VG, X_AV, X_OUT):
        left(plane_span, index)
    left(marks.at[pl.ds(0, NZ - 1)], X_MARK)
    left(stats.at[pl.ds(0, NZ - 1)], X_STAT); left(parts.at[pl.ds(0, NZ - 1)], X_PART)
    left(sums.at[pl.ds(0, NZ - 1)], X_SUM)
    left(grad_span, X_GRAD)
    left(grad_span, X_GRAD_B)


def body(queries, keys, values, out_grad):
    pair = jax.ShapeDtypeStruct((2, ROWS, D), BF16)
    anywhere = pl.BlockSpec(memory_space=pl.ANY)
    av, qk = pl.pallas_call(
        kernel,
        out_shape=(pair, pair),
        in_specs=[anywhere] * 4,
        out_specs=(anywhere, anywhere),
        scratch_shapes=[
            pltpu.VMEM((2, ROWS, D), BF16),
            pltpu.VMEM((2, ROWS, D), BF16),
            pltpu.VMEM((2, TOK, HD), BF16),
            pltpu.VMEM((2, TOK, HD), BF16),
            pltpu.VMEM((2, OWN, HD), BF16),
            pltpu.VMEM((NZ, 2, OWN, HD), BF16),
            pltpu.VMEM((NZ, 2 * SLAB, M), BF16),
            pltpu.VMEM((NZ, 2 * SLAB, M), BF16),
            pltpu.VMEM((2, M), F32),
            pltpu.VMEM((NZ, 2, M), F32),
            pltpu.VMEM((2 * SLAB, M), BF16),
            pltpu.VMEM((NZ, 2 * SLAB, M), BF16),
            pltpu.VMEM((2, TOK, HD), BF16),
            pltpu.VMEM((2, M, HD), BF16),
            pltpu.VMEM((2, NZ, OWN, HD), BF16),
            pltpu.VMEM((2, TOK, HD), BF16),
            pltpu.VMEM((TOK, M), F32),
            pltpu.VMEM((TOK, M), BF16),
            pltpu.VMEM((TOK, M), F32),
            pltpu.VMEM((4, HD, TOK), BF16),
            pltpu.VMEM((2, TOK, HD), F32),
            pltpu.VMEM((4, M, M), F32),
            pltpu.VMEM((ITERS + 1, 10, M, M), BF16),
            pltpu.SemaphoreType.REGULAR,
            pltpu.SemaphoreType.DMA((4,)),
            pltpu.SemaphoreType.DMA((10,)),
            pltpu.SemaphoreType.DMA((10,)),
        ],
        compiler_params=pltpu.CompilerParams(
            collective_id=0, has_side_effects=True, vmem_limit_bytes=63 * 1024 * 1024
        ),
    )(queries, keys, values, out_grad)
    return av[0], qk[0], qk[1], av[1]


def solution(mesh):
    spec = P(("seq", "head"), None)
    return jax.shard_map(body, mesh=mesh, in_specs=(spec,) * 4, out_specs=(spec,) * 4, check_vma=False)
```

```python
import functools

import jax
import jax.numpy as jnp
from jax import lax
from jax.experimental import pallas as pl
from jax.experimental.pallas import tpu as pltpu
from jax.sharding import PartitionSpec as P

MESH = pl.DeviceIdType.MESH
F32, BF16 = jnp.float32, jnp.bfloat16

NZ = 16
PLANE = 32
HEADS = 8
ROWS = 16
HD = 128
D = PLANE * HD
TOK = PLANE * ROWS
SEG = 32
OWN = TOK // SEG
M = NZ * OWN
SLAB = HD // NZ
ITERS = 6
SCALE = HD ** (-0.5)


def away(step, size):
    return min(step % size, -step % size)


NY, NX = 4, 4
PLANE_STEPS = sorted(
    ((i, j, k) for i in range(NY) for j in range(NX) for k in range(2) if i or j or k),
    key=lambda step: -away(step[0], NY) - away(step[1], NX),
)
CHIP_STEPS = [(i, j) for i, j, k in PLANE_STEPS if k == 0]
LINE_STEPS = sorted(range(1, NZ), key=lambda step: -away(step, NZ))

X_QK, X_VG, X_MARK, X_PART, X_SUM, X_AV, X_GRAD, X_OUT, X_STAT, X_GRAD_B = range(10)


def dot(left, right):
    return lax.dot_general(left, right, (((1,), (0,)), ((), ())), preferred_element_type=F32)


def dot_nt(left, right):
    return lax.dot_general(left, right, (((1,), (1,)), ((), ())), preferred_element_type=F32)


def split(x):
    high = x.astype(BF16)
    return high, (x - high.astype(F32)).astype(BF16)


def mul(left, right, product=dot):
    return product(left[0], right[0]) + (product(left[0], right[1]) + product(left[1], right[0]))


def mul_left(left, right, product=dot):
    return product(left, right[0]) + product(left, right[1])


def mul_right(left, right):
    return dot(left[0], right) + dot(left[1], right)


def kernel(
    q_ref, k_ref, v_ref, g_ref, av_ref, qk_ref,
    qk_in, vg_in, qk, vg, mark_out, marks, part_out, parts, stat_out, stats, sum_out, sums, av_out, grad_out, grads, qk_out,
    prob, low, kexp, trans, direct, square, saved, sync_sem, load_sem, send_sem, recv_sem,
):
    seq, head = lax.axis_index("seq"), lax.axis_index("head")
    y, z = seq // NZ, seq % NZ
    me = y * HEADS + head

    def plane_peer(rank):
        return (rank // HEADS * NZ + z, rank % HEADS)

    def line_peer(rank):
        return (y * NZ + rank, head)

    loads = [
        pltpu.make_async_copy(source, target, load_sem.at[index])
        for index, (source, target) in enumerate(
            ((q_ref, qk_in.at[0]), (k_ref, qk_in.at[1]), (v_ref, vg_in.at[0]), (g_ref, vg_in.at[1]))
        )
    ]
    for load in loads:
        load.start()

    barrier = pltpu.get_barrier_semaphore()
    core, x = head % 2, head // 2
    sibling = (seq, head + 1 - 2 * core)

    def greet(peer):
        pl.semaphore_signal(barrier, inc=1, device_id=peer, device_id_type=MESH)

    for i, j in CHIP_STEPS:
        greet(((y + i) % NY * NZ + z, (x + j) % NX * 2))
    greet(sibling)
    for step in LINE_STEPS:
        greet((y * NZ + (z + step) % NZ, 2 * x + 1))

    def met(first):
        @pl.when(core == first)
        def _():
            pl.semaphore_wait(barrier, PLANE - 1)
            pl.semaphore_signal(sync_sem, inc=1, device_id=sibling, device_id_type=MESH)

        @pl.when(core != first)
        def _():
            pl.semaphore_wait(sync_sem, 1)

    met(0)

    def send(source, target, index, peer):
        pltpu.make_async_remote_copy(
            src_ref=source, dst_ref=target, send_sem=send_sem.at[index], recv_sem=recv_sem.at[index],
            device_id=peer, device_id_type=MESH,
        ).start()

    def columns(rank):
        return pl.ds(pl.multiple_of(rank * HD, HD), HD)

    def rows(rank, count):
        return pl.ds(pl.multiple_of(rank * count, count), count)

    def plane_ranks():
        for i, j, k in PLANE_STEPS:
            yield (y + i) % NY * HEADS + (head // 2 + j) % NX * 2 + (head + k) % 2

    def scatter_heads(source, target, index):
        for peer in plane_ranks():
            send(source.at[:, :, columns(peer)], target.at[:, rows(me, ROWS), :], index, plane_peer(peer))

        target[:, rows(me, ROWS), :] = source[:, :, columns(me)]

    def return_to(peer, source, target, index):
        send(source.at[:, rows(peer, ROWS), :], target.at[:, :, columns(me)], index, plane_peer(peer))

    def own_block(source, target, index):
        return pltpu.make_async_copy(
            source.at[:, rows(me, ROWS), :], target.at[:, :, columns(me)], load_sem.at[index]
        )

    def over_line(source, target, index):
        for step in LINE_STEPS:
            peer = (z + step) % NZ
            send(source(peer), target.at[z], index, line_peer(peer))

    def arrived(span, index):
        pltpu.make_async_copy(span, span, recv_sem.at[index]).wait()

    def left(span, index):
        pltpu.make_async_copy(span, span, send_sem.at[index]).wait()

    loads[0].wait()
    loads[1].wait()
    scatter_heads(qk_in, qk, X_QK)
    plane_span = qk.at[:, pl.ds(0, TOK - ROWS), :]
    arrived(plane_span, X_QK)

    for index in range(2):
        summed = jnp.sum(qk[index].astype(F32).reshape(OWN, SEG, HD), axis=1)
        mark_out[index] = (summed * (1.0 / SEG)).astype(BF16)
    met(1)
    over_line(lambda peer: mark_out, marks, X_MARK)
    marks[z] = mark_out[...]
    loads[2].wait()
    loads[3].wait()
    scatter_heads(vg_in, vg, X_VG)
    for index in range(2):
        trans[index] = qk[index].T
    arrived(marks.at[pl.ds(0, NZ - 1)], X_MARK)
    mark_q = marks[:, 0].reshape(M, HD)
    mark_k = marks[:, 1].reshape(M, HD)

    scores = dot_nt(qk[1], mark_q)
    key_top = jnp.max(scores, axis=0, keepdims=True)
    exps = jnp.exp((scores - key_top) * SCALE)
    kexp[...] = exps
    key_sum = jnp.sum(exps, axis=0, keepdims=True)
    stat_out[0:1, :] = key_top
    stat_out[1:2, :] = key_sum
    over_line(lambda peer: stat_out, stats, X_STAT)
    stats[z] = stat_out[...]
    arrived(plane_span, X_VG)
    for index in range(2):
        trans[2 + index] = vg[index].T
    value_part = dot(trans[2], exps.astype(BF16))
    scores = dot_nt(qk[0], mark_k)
    top = jnp.max(scores, axis=1, keepdims=True)
    exps = jnp.exp((scores - top) * SCALE)
    token_prob = exps * (1.0 / jnp.sum(exps, axis=1, keepdims=True))
    prob[...] = token_prob
    token_low = token_prob.astype(BF16)
    low[...] = token_low
    mixing_part = dot(trans[3], token_low)
    pair = [value_part.reshape(NZ, SLAB, M), mixing_part.reshape(NZ, SLAB, M)]
    part_out[...] = jnp.concatenate(pair, axis=1).astype(BF16)
    over_line(lambda peer: part_out.at[peer], parts, X_PART)
    parts[z] = part_out[z]

    scores = dot_nt(mark_q, mark_k)
    exps = jnp.exp((scores - jnp.max(scores, axis=1, keepdims=True)) * SCALE)
    mark_prob = exps * (1.0 / jnp.sum(exps, axis=1, keepdims=True))
    square[0] = mark_prob
    factor = 1.0 / jnp.max(jnp.sum(mark_prob, axis=0, keepdims=True))
    square[1] = mark_prob.T * factor

    def keep(step, slot, value):
        saved[step, slot], saved[step, slot + 1] = split(value)

    def kept(step, slot):
        return saved[step, slot], saved[step, slot + 1]

    keep(ITERS, 8, mark_prob.T)

    @pl.loop(0, ITERS)
    def _(step):
        iterate = square[1]
        keep(step, 0, iterate)
        keep(step, 2, iterate.T)
        part = kept(step, 0)
        product = mul(split(square[0]), part)
        keep(step, 4, product)
        product_split = kept(step, 4)
        first = 7.0 * product - mul(product_split, product_split)
        keep(step, 6, first)
        second = 15.0 * product - mul(product_split, kept(step, 6))
        keep(step, 8, second)
        square[1] = 3.25 * iterate - 0.25 * mul(part, kept(step, 8))

    keep(ITERS, 0, square[1])

    arrived(stats.at[pl.ds(0, NZ - 1)], X_STAT)
    tops = [stats[peer, 0:1, :] for peer in range(NZ)]
    highest = functools.reduce(jnp.maximum, tops)
    weights = [jnp.exp((top - highest) * SCALE) for top in tops]
    total = sum(weight * stats[peer, 1:2, :] for peer, weight in enumerate(weights))
    inverse_total = 1.0 / total
    arrived(parts.at[pl.ds(0, NZ - 1)], X_PART)
    values, mixing_grad = 0.0, 0.0
    for peer in range(NZ):
        part = parts[peer].astype(F32)
        values = values + weights[peer] * part[0:SLAB]
        mixing_grad = mixing_grad + part[SLAB : 2 * SLAB]
    sum_out[...] = jnp.concatenate([values * inverse_total, mixing_grad], axis=0).astype(BF16)
    over_line(lambda peer: sum_out, sums, X_SUM)
    sums[z] = sum_out[...]
    key_prob = kexp[...] * (jnp.exp((key_top - highest) * SCALE) * inverse_total)
    kexp[...] = key_prob
    arrived(sums.at[pl.ds(0, NZ - 1)], X_SUM)
    both = sums[...].astype(F32)
    values = both[:, 0:SLAB, :].reshape(HD, M)
    values_low, mixing_grad = values.astype(BF16), both[:, SLAB : 2 * SLAB, :].reshape(HD, M).astype(BF16)
    inverse = kept(ITERS, 0)
    mixing_low = (mul_left(values_low, inverse, dot_nt)).astype(BF16)
    lv_low = (mul_left(mixing_grad, inverse)).astype(BF16)
    square[2] = jnp.zeros((M, M), F32)

    token_prob = prob[...]
    av_out[0] = dot_nt(low[...], mixing_low).astype(BF16)
    token_grad = dot(vg[1], mixing_low)
    dots = jnp.sum(token_grad * token_prob, axis=1, keepdims=True)
    token_sgrad = (token_prob * (token_grad - dots)).astype(BF16)
    direct[0] = dot(token_sgrad, mark_k) * SCALE
    grad_out[0] = (dot(trans[0], token_sgrad) * SCALE).astype(BF16).T
    over_line(lambda peer: grad_out.at[0, rows(peer, OWN), :], grads.at[0], X_GRAD)
    key_prob = kexp[...]
    av_out[1] = dot_nt(key_prob.astype(BF16), lv_low).astype(BF16)
    row_total = jnp.sum(lv_low.astype(F32) * values, axis=0, keepdims=True)
    key_dgrad = dot(vg[0], lv_low)
    key_sgrad = (key_prob * (key_dgrad - row_total)).astype(BF16)
    direct[1] = dot(key_sgrad, mark_q) * SCALE
    grad_out[1] = (dot(trans[1], key_sgrad) * SCALE).astype(BF16).T
    over_line(lambda peer: grad_out.at[1, rows(peer, OWN), :], grads.at[1], X_GRAD_B)
    for index in range(2):
        grads[index, z] = grad_out[index, rows(z, OWN), :]
    own_block(av_out, av_ref, 0).start()

    square[1] = dot(mixing_grad.T, values_low)
    square[3] = -0.25 * mul_right(kept(ITERS - 1, 2), square[1].astype(BF16))

    def step_back(step, before):
        second_grad = square[3]
        second_low = second_grad.astype(BF16)
        product_split = kept(step, 4)
        first_split = kept(step, 6)
        through = mul_right(product_split, second_low).astype(BF16)
        product_grad = 15.0 * second_grad - (mul_left(second_low, first_split) + mul_right(first_split, second_low))
        product_grad = (product_grad + mul_left(through, product_split)).astype(BF16)
        out_grad = square[1]
        out_grad = 3.25 * out_grad - 0.25 * mul_left(out_grad.astype(BF16), kept(step, 8))
        if before is not None:
            earlier = mul_right(kept(before, 2), out_grad.astype(BF16))
            square[3] = -0.25 * (earlier + mul_right(kept(before, 4), product_grad))
        square[1] = out_grad + mul_right(kept(ITERS, 8), product_grad)
        square[2] += mul_left(product_grad, kept(step, 0), dot_nt)

    step_back(ITERS - 1, ITERS - 2)
    for turn in range(3):
        return_to((me + 1 + turn) % PLANE, av_out, av_ref, X_AV)

    @pl.loop(1, ITERS - 1)
    def _(back):
        for turn in range(7):
            return_to((me + 4 + (back - 1) * 7 + turn) % PLANE, av_out, av_ref, X_AV)
        step_back(ITERS - 1 - back, ITERS - 2 - back)

    step_back(0, None)

    mark_grad = square[2] + square[1].T * factor
    mark_prob = square[0]
    mark_sgrad = mark_prob * (mark_grad - jnp.sum(mark_grad * mark_prob, axis=1, keepdims=True))
    square[1] = mark_sgrad
    square[2] = mark_sgrad.T
    grad_span = grads.at[0, pl.ds(0, NZ - 1)]
    arrived(grad_span, X_GRAD)
    arrived(grad_span, X_GRAD_B)
    from_query, from_key = split(square[1, rows(z, OWN), :]), split(square[2, rows(z, OWN), :])
    query_marks = (dot(from_query[0], mark_k) + dot(from_query[1], mark_k)) * SCALE
    key_marks = (dot(from_key[0], mark_q) + dot(from_key[1], mark_q)) * SCALE
    for peer in range(NZ):
        query_marks = query_marks + grads[1, peer].astype(F32)
        key_marks = key_marks + grads[0, peer].astype(F32)
    for index, total in ((0, query_marks), (1, key_marks)):
        spread = direct[index].reshape(OWN, SEG, HD) + (total * (1.0 / SEG))[:, None, :]
        qk_out[index] = spread.reshape(TOK, HD).astype(BF16)
    for peer in plane_ranks():
        return_to(peer, qk_out, qk_ref, X_OUT)
    own_block(qk_out, qk_ref, 1).start()

    out_span = av_ref.at[:, :, pl.ds(0, D - HD)]
    own_block(av_out, av_ref, 0).wait()
    own_block(qk_out, qk_ref, 1).wait()
    arrived(out_span, X_AV)
    arrived(out_span, X_OUT)
    for index in (X_QK, X_VG, X_AV, X_OUT):
        left(plane_span, index)
    left(marks.at[pl.ds(0, NZ - 1)], X_MARK)
    left(stats.at[pl.ds(0, NZ - 1)], X_STAT); left(parts.at[pl.ds(0, NZ - 1)], X_PART)
    left(sums.at[pl.ds(0, NZ - 1)], X_SUM)
    left(grad_span, X_GRAD)
    left(grad_span, X_GRAD_B)


def body(queries, keys, values, out_grad):
    pair = jax.ShapeDtypeStruct((2, ROWS, D), BF16)
    anywhere = pl.BlockSpec(memory_space=pl.ANY)
    av, qk = pl.pallas_call(
        kernel,
        out_shape=(pair, pair),
        in_specs=[anywhere] * 4,
        out_specs=(anywhere, anywhere),
        scratch_shapes=[
            pltpu.VMEM((2, ROWS, D), BF16),
            pltpu.VMEM((2, ROWS, D), BF16),
            pltpu.VMEM((2, TOK, HD), BF16),
            pltpu.VMEM((2, TOK, HD), BF16),
            pltpu.VMEM((2, OWN, HD), BF16),
            pltpu.VMEM((NZ, 2, OWN, HD), BF16),
            pltpu.VMEM((NZ, 2 * SLAB, M), BF16),
            pltpu.VMEM((NZ, 2 * SLAB, M), BF16),
            pltpu.VMEM((2, M), F32),
            pltpu.VMEM((NZ, 2, M), F32),
            pltpu.VMEM((2 * SLAB, M), BF16),
            pltpu.VMEM((NZ, 2 * SLAB, M), BF16),
            pltpu.VMEM((2, TOK, HD), BF16),
            pltpu.VMEM((2, M, HD), BF16),
            pltpu.VMEM((2, NZ, OWN, HD), BF16),
            pltpu.VMEM((2, TOK, HD), BF16),
            pltpu.VMEM((TOK, M), F32),
            pltpu.VMEM((TOK, M), BF16),
            pltpu.VMEM((TOK, M), F32),
            pltpu.VMEM((4, HD, TOK), BF16),
            pltpu.VMEM((2, TOK, HD), F32),
            pltpu.VMEM((4, M, M), F32),
            pltpu.VMEM((ITERS + 1, 10, M, M), BF16),
            pltpu.SemaphoreType.REGULAR,
            pltpu.SemaphoreType.DMA((4,)),
            pltpu.SemaphoreType.DMA((10,)),
            pltpu.SemaphoreType.DMA((10,)),
        ],
        compiler_params=pltpu.CompilerParams(
            collective_id=0, has_side_effects=True, vmem_limit_bytes=63 * 1024 * 1024
        ),
    )(queries, keys, values, out_grad)
    return av[0], qk[0], qk[1], av[1]


def solution(mesh):
    spec = P(("seq", "head"), None)
    return jax.shard_map(body, mesh=mesh, in_specs=(spec,) * 4, out_specs=(spec,) * 4, check_vma=False)
```
